256 devices in a mesh: frame: 2 (over core), tile: 128 (over z, x, y).
Axes of the slice: x: 4, y: 4, z: 8, core: 2. Of those that a mesh axis runs over, the one named last changes fastest.
Arguments:
- object_tiles: float32 [2, 128, 2, 256, 256], P('frame', 'tile'), may hold values from -5 to 5
- probe_field: float32 [2, 256, 256], replicated, may hold values from -5 to 5
- amplitudes: bfloat16 [2, 2048, 256, 256], P('frame', 'tile'), may hold values from 0.25 to 4
- offsets: int32 [2, 2048, 2], P('frame', 'tile'), may hold values from 0 to 255
- counts: int32 [2, 128], P('frame', 'tile'), may hold values from 1 to 16, 1024 in all within a row
Outputs:
- object_next: float32 [2, 128, 2, 256, 256], P('frame', 'tile')
The draws below stay inside these ranges and needn't reach their ends.
Inputs may be any that keep to these rules, and one draw needn't show every extreme that they name: Each frame's counts add up to 1024, and some tile of each frame has 16.
All inputs are finite; a program needn't handle non-finite values. No bound on the sum of `counts` on one device may be relied on, other than what follows from the above.
Results may differ from the reference program's by a relative error of at most 0.0042.
Values sent between devices are 32-bit elements; how exact they have to be, the bound alone decides.
A program may use at most 128 MiB of HBM per device.

```python
import math
import jax
import jax.numpy as jnp
import numpy as np
from jax import lax

PS = 256
TILE_COLS = 8
P_DEV = 16
P_MEAN = 8
FRAMES = 2
TILES = 128
PATTERNS = 2048


def touch_ends(array, stream_key, low, high):
    longest = array.shape.index(max(array.shape))
    spots = []
    for shift in (0, 1):
        where = [jax.random.randint(jax.random.fold_in(stream_key, axis), (), 0, length) for axis, length in enumerate(array.shape)]
        where[longest] = (where[longest] + shift) % array.shape[longest]
        spots.append(tuple(where))
    return array.at[spots[0]].set(low).at[spots[1]].set(high)


def level_of(own_key, dims, cuts, low, high):
    level = 1.0
    for axis_at, parts in cuts:
        steps = jax.random.uniform(jax.random.fold_in(jax.random.fold_in(own_key, 6), axis_at), (parts,), jnp.float32, low / len(cuts), high / len(cuts))
        level = level * jnp.repeat(jnp.exp(steps), dims[axis_at] // parts).reshape((-1,) + (1,) * (len(dims) - 1 - axis_at))
    return level


def split_up(count, total, reach, lean):
    portions = [(1 << 20) // math.isqrt(standing ** lean) + 1 for standing in range(2, count + 1)]
    rest, holding = total - reach - (count - 1), [1] * (count - 1)
    while rest > 0:
        movable = [i for i in range(count - 1) if holding[i] < reach]
        whole, budget = sum([portions[i] for i in movable]), rest
        for i in movable:
            extra = min(reach - holding[i], max(1, budget * portions[i] // whole), rest)
            holding[i] = holding[i] + extra
            rest = rest - extra
    return np.array([reach] + holding)


def uneven(stream_key, count, total, most, slope):
    if count == 2:
        one = jax.random.randint(stream_key, (), max(1, total - most), min(most, total - 1) + 1)
        return jnp.stack([one, total - one])
    sizes = jnp.asarray(split_up(count, total, most, slope), jnp.int32)
    couples = (count - 1) // 2
    donor, receiver = sizes[1:1 + 2 * couples:2], sizes[2:2 + 2 * couples:2]
    room = jnp.minimum(donor - 1, most - receiver)
    passed = jax.random.randint(jax.random.fold_in(stream_key, 1), (couples,), 0, 1 << 20) % (room + 1)
    sizes = sizes.at[1:1 + 2 * couples:2].set(donor - passed).at[2:2 + 2 * couples:2].set(receiver + passed)
    return sizes[jax.random.permutation(jax.random.fold_in(stream_key, 2), count)]


def bell_draw(key, shape, deviation, reach, cuts=(), held_as=jnp.bfloat16):
    result = deviation * jax.random.normal(key, shape, jnp.float32)
    if cuts:
        result = result * level_of(key, shape, cuts, -0.22, 0.18)
    return jnp.clip(result, -reach, reach).astype(held_as)


def setup_inputs(seed: int = 0) -> dict:
    keys = jax.random.split(jax.random.key(seed), 6)
    return {
        "object_tiles": bell_draw(keys[0], (FRAMES, TILES, 2, PS, PS), 0.7, 5.0, ((0, 2), (1, 128)), jnp.float32),
        "probe_field": bell_draw(keys[1], (2, PS, PS), 0.7, 5.0, (), jnp.float32),
        "amplitudes": jnp.clip(jnp.exp(math.log(4.0) - 2.7725887 * jax.random.uniform(keys[2], (FRAMES, PATTERNS, PS, PS), jnp.float32) ** level_of(keys[2], (FRAMES, PATTERNS, PS, PS), ((0, 2), (1, 128)), -0.2, 0.2)), 0.25, 4.0).astype(jnp.bfloat16),
        "offsets": touch_ends(jax.random.randint(keys[3], (FRAMES, PATTERNS, 2), 0, PS), jax.random.fold_in(keys[3], 1), 0, PS - 1).astype(jnp.int32),
        "counts": jax.vmap(lambda own: uneven(own, TILES, P_MEAN * TILES, P_DEV, 2))(jax.random.split(keys[4], FRAMES)).reshape((FRAMES, TILES)).astype(jnp.int32),
    }


damping = 0.1
variation_weight = 0.2
smoothing = 0.25
modulus_floor = 0.5

def dft_tables(tile_side):
    numbers = jnp.arange(tile_side, dtype=jnp.int32)
    phases = (numbers[:, None] * numbers[None, :] % tile_side).astype(jnp.float32) * (2.0 * math.pi / tile_side)
    factor = 1.0 / math.sqrt(tile_side)
    cosine = jnp.cos(phases) * factor
    minus_sine = -jnp.sin(phases) * factor
    first_table = jnp.stack([jnp.stack([cosine, -minus_sine]), jnp.stack([minus_sine, cosine])]).astype(jnp.bfloat16)
    second_table = jnp.stack([jnp.stack([cosine, minus_sine]), jnp.stack([-minus_sine, cosine])]).astype(jnp.bfloat16)
    return (first_table, second_table)

def transform(signal, first_table, second_table):
    signal = lax.optimization_barrier(signal)
    halfway = jnp.einsum('oijm,simk->sojk', first_table.astype(jnp.float32), signal.astype(jnp.float32)).astype(jnp.bfloat16)
    halfway = lax.optimization_barrier(halfway)
    return jnp.einsum('sijm,iomk->sojk', halfway.astype(jnp.float32), second_table.astype(jnp.float32))

def fit_terms(patches, probe_field, measured, in_use, first_table, second_table):
    probe_re = probe_field[0]
    probe_im = probe_field[1]
    part_re = patches[:, 0]
    part_im = patches[:, 1]
    exit_wave = jnp.stack([probe_re * part_re - probe_im * part_im, probe_re * part_im + probe_im * part_re], 1).astype(jnp.bfloat16)
    farfield = transform(exit_wave, first_table, second_table)
    modulus = jnp.sqrt(farfield[:, 0] ** 2 + farfield[:, 1] ** 2)
    retained = 1.0 - measured.astype(jnp.float32) / jnp.maximum(modulus, modulus_floor)
    mismatch = (farfield * retained[:, None]).astype(jnp.bfloat16)
    nearfield = transform(mismatch, second_table, first_table)
    grad_re = probe_re * nearfield[:, 0] + probe_im * nearfield[:, 1]
    grad_im = probe_re * nearfield[:, 1] - probe_im * nearfield[:, 0]
    lighting = jnp.broadcast_to(probe_re ** 2 + probe_im ** 2, grad_re.shape)
    return jnp.stack([grad_re, grad_im, lighting], 1) * in_use[:, None, None, None]

def reference(object_tiles, probe_field, amplitudes, offsets, counts):
    frame_count = object_tiles.shape[0]
    tile_count = object_tiles.shape[1]
    tile_side = object_tiles.shape[-1]
    slot_count = amplitudes.shape[1] // tile_count
    tile_rows = tile_count // TILE_COLS
    height = tile_rows * tile_side
    width = TILE_COLS * tile_side
    object_image = object_tiles.reshape(frame_count, tile_rows, TILE_COLS, 2, tile_side, tile_side)
    object_image = object_image.transpose(0, 3, 1, 4, 2, 5).reshape(frame_count, 2, height, width)
    padded = jnp.pad(object_image, ((0, 0), (0, 0), (0, tile_side), (0, tile_side)))
    first_table, second_table = dft_tables(tile_side)
    anchor = jnp.zeros((), jnp.int32)

    def one_tile(step_index, gradients):
        step_index = jnp.asarray(step_index).astype(jnp.int32)
        frame_index = step_index // tile_count
        tile_index = step_index % tile_count
        base_row = tile_index // TILE_COLS * tile_side
        base_col = tile_index % TILE_COLS * tile_side
        frame_offsets = lax.dynamic_index_in_dim(offsets, frame_index, 0, keepdims=False)
        corners = lax.dynamic_slice_in_dim(frame_offsets, tile_index * slot_count, slot_count, 0).astype(jnp.int32)
        frame_amps = lax.dynamic_index_in_dim(amplitudes, frame_index, 0, keepdims=False)
        measured = lax.dynamic_slice_in_dim(frame_amps, tile_index * slot_count, slot_count, 0)
        picture = lax.dynamic_index_in_dim(padded, frame_index, 0, keepdims=False)

        def extract(corner):
            return lax.dynamic_slice(picture, (anchor, base_row + corner[0], base_col + corner[1]), (2, tile_side, tile_side))
        patches = jax.vmap(extract)(corners)
        limit = counts[frame_index, tile_index].astype(jnp.int32)
        in_use = (jnp.arange(slot_count, dtype=jnp.int32) < limit).astype(jnp.float32)
        pieces = fit_terms(patches, probe_field, measured, in_use, first_table, second_table)
        layer_grad = lax.dynamic_index_in_dim(gradients, frame_index, 0, keepdims=False)

        def deposit(slot_index, accumulated):
            slot_index = jnp.asarray(slot_index).astype(jnp.int32)
            start_at = (anchor, base_row + corners[slot_index, 0], base_col + corners[slot_index, 1])
            current = lax.dynamic_slice(accumulated, start_at, (3, tile_side, tile_side))
            addition = lax.dynamic_index_in_dim(pieces, slot_index, 0, keepdims=False)
            return lax.dynamic_update_slice(accumulated, current + addition, start_at)
        layer_grad = lax.fori_loop(0, slot_count, deposit, layer_grad)
        return lax.dynamic_update_index_in_dim(gradients, layer_grad, frame_index, 0)
    gradients = jnp.zeros((frame_count, 3, height + tile_side, width + tile_side), jnp.float32)
    gradients = lax.fori_loop(0, frame_count * tile_count, one_tile, gradients)
    fit_total = gradients[:, :, :height, :width]
    diff_x = jnp.concatenate([object_image[..., 1:] - object_image[..., :-1], jnp.zeros((frame_count, 2, height, 1), jnp.float32)], 3)
    diff_y = jnp.concatenate([object_image[:, :, 1:, :] - object_image[:, :, :-1, :], jnp.zeros((frame_count, 2, 1, width), jnp.float32)], 2)
    spatial = lax.optimization_barrier(jnp.sum(diff_x ** 2 + diff_y ** 2, 1))
    diff_t = object_image[1] - object_image[0]
    time_change = lax.optimization_barrier(jnp.sum(diff_t ** 2, 0))
    first_weight = 1.0 / jnp.sqrt(spatial[0] + time_change + smoothing)
    second_weight = 1.0 / jnp.sqrt(spatial[1] + time_change + smoothing)
    weight = jnp.stack([first_weight, second_weight])[:, None]
    flow_x = weight * diff_x
    flow_y = weight * diff_y
    grad_x = jnp.concatenate([jnp.zeros((frame_count, 2, height, 1), jnp.float32), flow_x[..., :-1]], 3) - flow_x
    grad_y = jnp.concatenate([jnp.zeros((frame_count, 2, 1, width), jnp.float32), flow_y[:, :, :-1, :]], 2) - flow_y
    flow_t = (first_weight + second_weight) * diff_t
    grad_t = jnp.stack([-flow_t, flow_t])
    probe_power = jnp.max(probe_field[0] ** 2 + probe_field[1] ** 2)
    updated = object_image - fit_total[:, :2] / (fit_total[:, 2:] + damping * probe_power + 1e-06) - variation_weight * (grad_x + grad_y + grad_t)
    updated = updated.reshape(frame_count, 2, tile_rows, tile_side, TILE_COLS, tile_side).transpose(0, 2, 4, 1, 3, 5)
    return updated.reshape(frame_count, tile_count, 2, tile_side, tile_side)
```

```python
import functools
import math

import jax
import jax.numpy as jnp
import numpy as np
from jax import lax
from jax.experimental import pallas as pl
from jax.experimental.pallas import tpu as pltpu
from jax.sharding import PartitionSpec as P

TILE_COLS = 8
SIDE = 256
HALF = 128
CHUNK = 32
F32, BF16 = jnp.float32, jnp.bfloat16
MESH = pl.DeviceIdType.MESH

damping = 0.1
variation_weight = 0.2
smoothing = 0.25


class Place:
    def __init__(self):
        self.frame = lax.axis_index("frame")
        self.tile = lax.axis_index("tile")
        tile_rows = lax.axis_size("tile") // TILE_COLS
        column = self.tile % TILE_COLS
        row = self.tile // TILE_COLS
        self.left = column > 0
        self.right = column < TILE_COLS - 1
        self.up = row > 0
        self.down = row < tile_rows - 1

    def at(self, step):
        return (self.frame, self.tile + step)

    def neighbours(self):
        return (
            (self.left, -1),
            (self.right, 1),
            (self.up, -TILE_COLS),
            (self.down, TILE_COLS),
        )


def both(a, b):
    return jnp.logical_and(a, b)


def greet(place, partner=None):
    barrier = pltpu.get_barrier_semaphore()
    total = jnp.int32(0)
    for there, step in place.neighbours():
        total = total + there.astype(jnp.int32)

        @pl.when(there)
        def _(step=step):
            pl.semaphore_signal(barrier, inc=1, device_id=place.at(step), device_id_type=MESH)

    if partner is not None:
        total = total + 1
        pl.semaphore_signal(barrier, inc=1, device_id=partner, device_id_type=MESH)
    return lambda: pl.semaphore_wait(barrier, total)


class Sent:
    def __init__(self, source, target, device, sems, index, sends, receives):
        send_sem, recv_sem = sems
        self.copy = lambda: pltpu.make_async_remote_copy(
            src_ref=source,
            dst_ref=target,
            send_sem=send_sem.at[index],
            recv_sem=recv_sem.at[index],
            device_id=device,
            device_id_type=MESH,
        )
        self.sends, self.receives = sends, receives

    def start(self):
        @pl.when(self.sends)
        def _():
            self.copy().start()

    def wait_recv(self):
        @pl.when(self.receives)
        def _():
            self.copy().wait_recv()

    def wait_send(self):
        @pl.when(self.sends)
        def _():
            self.copy().wait_send()


def halo_kernel(
    tile_ref, meta_ref, region, metas, packed, blank, meta_blank, local_sem, blank_sem, send_sem, recv_sem
):
    place = Place()
    all_here = greet(place)
    sems = (send_sem, recv_sem)
    for b in range(2):
        packed[b] = tile_ref[:, :, b * HALF : (b + 1) * HALF]
    blank[...] = jnp.zeros_like(blank)
    meta_blank[...] = jnp.zeros_like(meta_blank)
    upper, lower = pl.ds(0, SIDE), pl.ds(SIDE, SIDE)

    own = [
        pltpu.make_async_copy(packed.at[b], region.at[b, :, upper], local_sem.at[b]) for b in range(2)
    ]
    own.append(pltpu.make_async_copy(meta_ref, metas.at[0], local_sem.at[2]))
    for copy in own:
        copy.start()
    corner_there = both(place.right, place.down)
    above_there = both(place.left, place.up)
    blanks = []
    for b in range(2):
        for there, column, rows in (
            (place.right, 2 + b, upper),
            (place.down, b, lower),
            (corner_there, 2 + b, lower),
        ):
            blanks.append((there, blank, region.at[column, :, rows]))
    for i, there in enumerate((place.left, place.up, above_there)):
        blanks.append((there, meta_blank, metas.at[1 + i]))
    blanks = [
        (there, pltpu.make_async_copy(source, target, blank_sem.at[i]))
        for i, (there, source, target) in enumerate(blanks)
    ]
    for there, copy in blanks:
        pl.when(jnp.logical_not(there))(copy.start)

    to_up = [
        Sent(packed.at[b], region.at[b, :, lower], place.at(-TILE_COLS), sems, b, place.up, place.down)
        for b in range(2)
    ]
    to_left = [
        Sent(packed.at[b], region.at[2 + b, :, upper], place.at(-1), sems, 2 + b, place.left, place.right)
        for b in range(2)
    ]
    relay_left = Sent(
        region.at[0, :, lower], region.at[2, :, lower], place.at(-1), sems, 4,
        both(place.left, place.down), corner_there,
    )
    relay_up = Sent(
        region.at[3, :, upper], region.at[3, :, lower], place.at(-TILE_COLS), sems, 5,
        both(place.up, place.right), corner_there,
    )
    meta_right = Sent(meta_ref, metas.at[1], place.at(1), sems, 6, place.right, place.left)
    meta_down = Sent(meta_ref, metas.at[2], place.at(TILE_COLS), sems, 7, place.down, place.up)
    meta_relay = Sent(
        metas.at[1], metas.at[3], place.at(TILE_COLS), sems, 8, both(place.down, place.left), above_there
    )

    all_here()
    meta_right.start()
    meta_down.start()
    to_up[0].start()
    to_left[1].start()
    to_up[1].start()
    to_left[0].start()
    meta_right.wait_recv()
    meta_relay.start()
    to_up[0].wait_recv()
    relay_left.start()
    to_left[1].wait_recv()
    relay_up.start()
    for copy in own:
        copy.wait()
    for there, copy in blanks:
        pl.when(jnp.logical_not(there))(copy.wait)
    for sent in (to_up[1], to_left[0], relay_left, relay_up, meta_down, meta_relay):
        sent.wait_recv()
    for sent in (*to_up, *to_left, relay_left, relay_up, meta_right, meta_down, meta_relay):
        sent.wait_send()


def halo(tile, meta):
    V = pl.BlockSpec(memory_space=pltpu.VMEM)
    return pl.pallas_call(
        halo_kernel,
        out_shape=(
            jax.ShapeDtypeStruct((4, 2, 2 * SIDE, HALF), F32),
            jax.ShapeDtypeStruct((4, 8, HALF), jnp.int32),
        ),
        in_specs=[V, V],
        out_specs=(pl.BlockSpec(memory_space=pl.ANY), pl.BlockSpec(memory_space=pl.ANY)),
        scratch_shapes=[
            pltpu.VMEM((2, 2, SIDE, HALF), F32),
            pltpu.VMEM((2, SIDE, HALF), F32),
            pltpu.VMEM((8, HALF), jnp.int32),
            pltpu.SemaphoreType.DMA((3,)),
            pltpu.SemaphoreType.DMA((9,)),
            pltpu.SemaphoreType.DMA((9,)),
            pltpu.SemaphoreType.DMA((9,)),
        ],
        compiler_params=pltpu.CompilerParams(
            collective_id=0, has_side_effects=True, vmem_limit_bytes=40 << 20
        ),
        name="halo",
    )(tile, meta)


def dft_blocks():
    numbers = np.arange(SIDE)
    phases = (np.outer(numbers, numbers) % SIDE) * (2.0 * math.pi / SIDE)
    cosine = np.cos(phases) / math.sqrt(SIDE)
    minus_sine = -np.sin(phases) / math.sqrt(SIDE)
    forward = np.block([[cosine, -minus_sine], [minus_sine, cosine]])
    backward = np.block([[cosine, minus_sine], [-minus_sine, cosine]])
    return jnp.asarray(forward, BF16), jnp.asarray(backward, BF16)


def fit_kernel(
    count_ref, corner_ref, region_ref, probe_ref, amps_ref, fwd_ref, bwd_ref,
    left_ref, right_ref, rolled, wave, half, far, zero_dummy=None,
):
    count = count_ref[0, 0]
    left_ref[...] = jnp.zeros_like(left_ref)
    right_ref[...] = jnp.zeros_like(right_ref)
    lanes = lax.broadcasted_iota(jnp.int32, (CHUNK, SIDE), 1)
    steps = SIDE // CHUNK
    pairs = (count + 1) // 2

    def make_wave(pair):
        for k in range(2):
            slot = 2 * pair + k
            row, col = corner_ref[slot, 0], corner_ref[slot, 1]
            inside = lanes >= col
            for step in range(steps):
                here = pl.ds(step * CHUNK, CHUNK)
                there = pl.ds(row + step * CHUNK, CHUNK)
                probe_re = pltpu.roll(probe_ref[0, here, :], col, 1)
                probe_im = pltpu.roll(probe_ref[1, here, :], col, 1)
                rolled[k, 0, here, :] = probe_re
                rolled[k, 1, here, :] = probe_im
                part = []
                for c in range(2):
                    near = jnp.concatenate([region_ref[0, c, there, :], region_ref[1, c, there, :]], 1)
                    wide = jnp.concatenate([region_ref[2, c, there, :], region_ref[3, c, there, :]], 1)
                    part.append(jnp.where(inside, near, wide))
                cols = pl.ds(k * SIDE, SIDE)
                wave[here, cols] = (probe_re * part[0] - probe_im * part[1]).astype(BF16)
                wave[pl.ds(SIDE + step * CHUNK, CHUNK), cols] = (
                    probe_re * part[1] + probe_im * part[0]
                ).astype(BF16)

    def transform(first, second):
        for k in range(2):
            cols = pl.ds(k * SIDE, SIDE)
            for c in range(2):
                rows = pl.ds(c * SIDE, SIDE)
                half[cols, rows] = jnp.dot(
                    first[rows, :], wave[:, cols], preferred_element_type=F32
                ).astype(BF16)
        for c in range(2):
            cols = pl.ds(c * SIDE, SIDE)
            far[c] = jnp.dot(half[...], second[:, cols], preferred_element_type=F32)

    def correct(pair):
        for k in range(2):
            cols = pl.ds(k * SIDE, SIDE)
            for step in range(steps):
                here = pl.ds(step * CHUNK, CHUNK)
                there = pl.ds(k * SIDE + step * CHUNK, CHUNK)
                far_re, far_im = far[0, there, :], far[1, there, :]
                measured = amps_ref[2 * pair + k, here, :].astype(F32)
                inverse = jnp.minimum(lax.rsqrt(far_re * far_re + far_im * far_im), 2.0)
                retained = 1.0 - measured * inverse
                wave[here, cols] = (far_re * retained).astype(BF16)
                wave[pl.ds(SIDE + step * CHUNK, CHUNK), cols] = (far_im * retained).astype(BF16)

    def deposit(pair):
        for k in range(2):
            slot = 2 * pair + k
            row, col = corner_ref[slot, 0], corner_ref[slot, 1]
            used = slot < count
            inside = lanes >= jnp.where(used, col, 2 * SIDE)
            outside = lanes < jnp.where(used, col, 0)
            for step in range(steps):
                here = pl.ds(step * CHUNK, CHUNK)
                there = pl.ds(row + step * CHUNK, CHUNK)
                from_ = pl.ds(k * SIDE + step * CHUNK, CHUNK)
                near_re, near_im = far[0, from_, :], far[1, from_, :]
                probe_re, probe_im = rolled[k, 0, here, :], rolled[k, 1, here, :]
                grads = (
                    probe_re * near_re + probe_im * near_im,
                    probe_re * near_im - probe_im * near_re,
                )
                for c in range(2):
                    near = jnp.where(inside, grads[c], 0.0)
                    wide = jnp.where(outside, grads[c], 0.0)
                    for b in range(2):
                        cols = slice(b * HALF, (b + 1) * HALF)
                        left_ref[b, c, there, :] += near[:, cols]
                        right_ref[b, c, there, :] += wide[:, cols]

    def body(pair, carry):
        make_wave(pair)
        transform(fwd_ref, bwd_ref)
        correct(pair)
        transform(bwd_ref, fwd_ref)
        deposit(pair)
        return carry

    lax.fori_loop(0, pairs, body, 0)


def fit(counts, corners, region, probe, amps):
    fwd, bwd = dft_blocks()
    V = pl.BlockSpec(memory_space=pltpu.VMEM)
    S = pl.BlockSpec(memory_space=pltpu.SMEM)
    shape = jax.ShapeDtypeStruct((2, 2, 2 * SIDE, HALF), F32)
    return pl.pallas_call(
        fit_kernel,
        out_shape=(shape, shape),
        in_specs=[S, S, V, V, V, V, V],
        out_specs=(V, V),
        scratch_shapes=[
            pltpu.VMEM((2, 2, SIDE, SIDE), F32),
            pltpu.VMEM((2 * SIDE, 2 * SIDE), BF16),
            pltpu.VMEM((2 * SIDE, 2 * SIDE), BF16),
            pltpu.VMEM((2, 2 * SIDE, SIDE), F32),
        ],
        compiler_params=pltpu.CompilerParams(vmem_limit_bytes=40 << 20),
        name="fit",
    )(counts, corners, region, probe, amps, fwd, bwd)


def join_kernel(
    metas, tile_ref, region, left_ref, right_ref, probe_ref, out_ref,
    corner, from_left, from_up, partner_tile, weights, rims, edge_right, edge_down,
    power, lighting, flow_x, flow_y, local_sem, send_sem, recv_sem,
):
    place = Place()
    partner = (1 - place.frame, place.tile)
    all_here = greet(place, partner)
    sems = (send_sem, recv_sem)
    always = place.tile >= 0
    upper, lower = pl.ds(0, SIDE), pl.ds(SIDE, SIDE)
    edges = (
        pltpu.make_async_copy(region.at[2, :, upper], edge_right, local_sem.at[0]),
        pltpu.make_async_copy(region.at[pl.ds(0, 2), :, pl.ds(SIDE, 8)], edge_down, local_sem.at[1]),
    )
    for copy in edges:
        copy.start()

    out_there = both(place.right, place.down)
    right, down = place.at(1), place.at(TILE_COLS)
    corner_right = Sent(
        right_ref.at[0, :, lower], corner.at[0], right, sems, 0, out_there, both(place.left, place.down)
    )
    corner_down = Sent(
        right_ref.at[1, :, lower], corner.at[1], down, sems, 1, out_there, both(place.up, place.right)
    )
    plain_right = Sent(
        right_ref.at[0, :, upper], from_left.at[0], right, sems, 2, place.right, place.left
    )
    plain_down = Sent(left_ref.at[1, :, lower], from_up.at[1], down, sems, 3, place.down, place.up)
    merged_down = Sent(corner.at[0], from_up.at[0], down, sems, 4, place.down, place.up)
    merged_right = Sent(corner.at[1], from_left.at[1], right, sems, 5, place.right, place.left)
    tile_over = Sent(tile_ref, partner_tile, partner, sems, 6, always, always)
    weight_over = Sent(weights.at[0], weights.at[1], partner, sems, 7, always, always)
    rim_right = Sent(rims.at[0], rims.at[1], right, sems, 8, place.right, place.left)
    rim_down = Sent(rims.at[2], rims.at[3], down, sems, 9, place.down, place.up)

    all_here()
    tile_over.start()
    corner_right.start()
    corner_down.start()
    plain_right.start()
    plain_down.start()

    @pl.when(jnp.logical_not(place.left))
    def _():
        from_left[...] = jnp.zeros_like(from_left)
        rims[1] = jnp.zeros((8, SIDE), F32)

    @pl.when(jnp.logical_not(place.up))
    def _():
        from_up[...] = jnp.zeros_like(from_up)
        rims[3] = jnp.zeros((8, SIDE), F32)

    rims[0] = jnp.zeros((8, SIDE), F32)
    rims[2] = jnp.zeros((8, SIDE), F32)

    for copy in edges:
        copy.wait()
    tile_over.wait_recv()
    lanes = lax.broadcasted_iota(jnp.int32, (SIDE, SIDE), 1)
    rows = lax.broadcasted_iota(jnp.int32, (SIDE, SIDE), 0)
    x_lives = jnp.logical_or(lanes < SIDE - 1, place.right)
    y_lives = jnp.logical_or(rows < SIDE - 1, place.down)
    total = jnp.full((SIDE, SIDE), smoothing, F32)
    for c in range(2):
        centre = tile_ref[c]
        beyond = pltpu.roll(edge_right[c], HALF - 1, 1)
        ahead = jnp.where(
            lanes == SIDE - 1, jnp.concatenate([beyond, beyond], 1), pltpu.roll(centre, SIDE - 1, 1)
        )
        diff_x = jnp.where(x_lives, ahead - centre, 0.0)
        below = jnp.concatenate([edge_down[0, c, 0:1, :], edge_down[1, c, 0:1, :]], 1)
        ahead = jnp.where(
            rows == SIDE - 1, jnp.broadcast_to(below, (SIDE, SIDE)), pltpu.roll(centre, SIDE - 1, 0)
        )
        diff_y = jnp.where(y_lives, ahead - centre, 0.0)
        diff_t = partner_tile[c] - centre
        flow_x[c] = diff_x
        flow_y[c] = diff_y
        total = total + diff_x * diff_x + diff_y * diff_y + diff_t * diff_t
    weight = lax.rsqrt(total)
    weights[0] = weight
    weight_over.start()
    for c in range(2):
        flow = weight * flow_x[c]
        flow_x[c] = flow
        rims[0, c : c + 1, :] = flow[:, HALF:].T[HALF - 1 : HALF, :]
        flow = weight * flow_y[c]
        flow_y[c] = flow
        rims[2, c : c + 1, :] = flow[SIDE - 1 : SIDE, :]
    rim_right.start()
    rim_down.start()

    lighted = probe_ref[0] * probe_ref[0] + probe_ref[1] * probe_ref[1]
    floor = damping * jnp.max(lighted) + 1e-6
    power[...] = jnp.zeros_like(power)
    for b in range(2):
        power[b, lower, :] = lighted[:, b * HALF : (b + 1) * HALF]
    lighting[...] = jnp.zeros_like(lighting)
    chunk_lanes = lax.broadcasted_iota(jnp.int32, (CHUNK, SIDE), 1)

    def lamp(number, carry):
        source, slot = number // SLOTS, number % SLOTS
        row, col = metas[source, 0, slot], metas[source, 1, slot]
        used = slot < metas[source, 2, 0]
        beside = source % 2 == 1
        start = SIDE + SIDE * (source // 2) - row
        low = jnp.where(beside, 0, jnp.where(used, col, 2 * SIDE))
        high = jnp.where(beside, jnp.where(used, col, 0), 2 * SIDE)
        lit = both(chunk_lanes >= low, chunk_lanes < high)
        for step in range(SIDE // CHUNK):
            here = pl.ds(step * CHUNK, CHUNK)
            there = pl.ds(start + step * CHUNK, CHUNK)
            light = jnp.concatenate([power[0, there, :], power[1, there, :]], 1)
            lighting[here, :] += jnp.where(lit, pltpu.roll(light, col, 1), 0.0)
        return carry

    def merge(index, sent, out, there, came, addend):
        sent.wait_recv()

        @pl.when(both(there, came))
        def _():
            corner[index] += addend

        @pl.when(both(there, jnp.logical_not(came)))
        def _():
            corner[index] = addend

        out.start()

    lax.fori_loop(0, SLOTS, lamp, 0)
    merge(0, corner_right, merged_down, place.down, place.left, left_ref[0, :, lower])
    merge(1, corner_down, merged_right, place.right, place.up, right_ref[1, :, upper])
    lax.fori_loop(SLOTS, 4 * SLOTS, lamp, 0)

    weight_over.wait_recv()
    rim_right.wait_recv()
    rim_down.wait_recv()
    for sent in (plain_right, plain_down, merged_down, merged_right):
        sent.wait_recv()
    for c in range(2):
        centre = tile_ref[c]
        diff_t = partner_tile[c] - centre
        rim = jnp.broadcast_to(rims[1, c : c + 1, :], (HALF, SIDE)).T
        rim = jnp.concatenate([rim, rim], 1)
        flow = flow_x[c]
        grad = jnp.where(lanes == 0, rim, pltpu.roll(flow, 1, 1)) - flow
        rim = jnp.broadcast_to(rims[3, c : c + 1, :], (SIDE, SIDE))
        flow = flow_y[c]
        grad = grad + jnp.where(rows == 0, rim, pltpu.roll(flow, 1, 0)) - flow
        grad = grad - (weights[0] + weights[1]) * diff_t
        fit = jnp.concatenate(
            [left_ref[b, c, upper, :] + from_left[b, c] + from_up[b, c] for b in range(2)], 1
        )
        out_ref[c] = centre - fit / (lighting[...] + floor) - variation_weight * grad
    for sent in (
        corner_right, corner_down, plain_right, plain_down, merged_down, merged_right,
        tile_over, weight_over, rim_right, rim_down,
    ):
        sent.wait_send()


SLOTS = 16


def join(metas, tile, region, left, right, probe):
    V = pl.BlockSpec(memory_space=pltpu.VMEM)
    S = pl.BlockSpec(memory_space=pltpu.SMEM)
    block = (2, SIDE, HALF)
    return pl.pallas_call(
        join_kernel,
        out_shape=jax.ShapeDtypeStruct((2, SIDE, SIDE), F32),
        in_specs=[S, V, pl.BlockSpec(memory_space=pl.ANY), V, V, V],
        out_specs=V,
        scratch_shapes=[
            pltpu.VMEM((2, *block), F32),
            pltpu.VMEM((2, *block), F32),
            pltpu.VMEM((2, *block), F32),
            pltpu.VMEM((2, SIDE, SIDE), F32),
            pltpu.VMEM((2, SIDE, SIDE), F32),
            pltpu.VMEM((4, 8, SIDE), F32),
            pltpu.VMEM(block, F32),
            pltpu.VMEM((2, 2, 8, HALF), F32),
            pltpu.VMEM((2, 3 * SIDE, HALF), F32),
            pltpu.VMEM((SIDE, SIDE), F32),
            pltpu.VMEM((2, SIDE, SIDE), F32),
            pltpu.VMEM((2, SIDE, SIDE), F32),
            pltpu.SemaphoreType.DMA((2,)),
            pltpu.SemaphoreType.DMA((10,)),
            pltpu.SemaphoreType.DMA((10,)),
        ],
        compiler_params=pltpu.CompilerParams(
            collective_id=1, has_side_effects=True, vmem_limit_bytes=40 << 20
        ),
        name="join",
    )(metas, tile, region, left, right, probe)


def local(object_tiles, probe_field, amplitudes, offsets, counts):
    tile = object_tiles[0, 0]
    slots = amplitudes.shape[1]
    meta = jnp.zeros((8, HALF), jnp.int32)
    meta = meta.at[0:2, :slots].set(offsets[0].T).at[2, 0].set(counts[0, 0])
    region, metas = halo(tile, meta)
    left, right = fit(counts, offsets[0], region, probe_field, amplitudes[0])
    return join(metas, tile, region, left, right, probe_field)[None, None]


def solution(mesh):
    return jax.shard_map(
        local,
        mesh=mesh,
        in_specs=(
            P("frame", "tile", None, None, None),
            P(),
            P("frame", "tile", None, None),
            P("frame", "tile", None),
            P("frame", "tile"),
        ),
        out_specs=P("frame", "tile", None, None, None),
        check_vma=False,
    )
```

```python
import functools
import math

import jax
import jax.numpy as jnp
import numpy as np
from jax import lax
from jax.experimental import pallas as pl
from jax.experimental.pallas import tpu as pltpu
from jax.sharding import PartitionSpec as P

TILE_COLS = 8
SIDE = 256
HALF = 128
CHUNK = 32
PIECES = 4
LAG = 3
LAG2 = 2
F32, BF16 = jnp.float32, jnp.bfloat16
MESH = pl.DeviceIdType.MESH

damping = 0.1
variation_weight = 0.2
smoothing = 0.25


def both(a, b):
    return jnp.logical_and(a, b)


class Place:
    def __init__(self):
        self.frame = lax.axis_index("frame")
        self.tile = lax.axis_index("tile")
        self.tiles = lax.axis_size("tile")
        column, row = self.tile % TILE_COLS, self.tile // TILE_COLS
        self.left = column > 0
        self.right = column < TILE_COLS - 1
        self.up = row > 0
        self.down = row < self.tiles // TILE_COLS - 1

    def holds(self, source, step):
        tile = self.tile - step
        there = both(tile >= 0, tile < self.tiles)
        return both(there, source(tile % TILE_COLS, tile // TILE_COLS, self.tiles // TILE_COLS))

    def greet(self, routes, partner=None):
        barrier = pltpu.get_barrier_semaphore()
        before, after = {}, {}
        for route in routes:
            for h, step in enumerate(route.hops):
                for known, role in ((after, route.roles[h]), (before, route.roles[h + 1])):
                    known[step] = jnp.logical_or(known[step], role) if step in known else role
        for step, there in before.items():

            @pl.when(there)
            def _(step=step):
                device = (self.frame, self.tile - step)
                pl.semaphore_signal(barrier, inc=1, device_id=device, device_id_type=MESH)

        total = jnp.int32(0)
        for there in after.values():
            total = total + there.astype(jnp.int32)
        if partner is not None:
            total = total + 1
            pl.semaphore_signal(barrier, inc=1, device_id=partner, device_id_type=MESH)
        return lambda: pl.semaphore_wait(barrier, total)


class Route:
    def __init__(self, place, sems, index, hops, source, origin, target, relays=()):
        assert len(relays) == len(hops) - 1
        steps = [sum(hops[:h]) for h in range(len(hops) + 1)]
        self.hops = hops
        self.roles = [place.holds(source, step) for step in steps]
        stops = [origin, *relays, target]
        self.copies = [
            functools.partial(
                pltpu.make_async_remote_copy,
                src_ref=stops[h],
                dst_ref=stops[h + 1],
                send_sem=sems[0].at[index + h],
                recv_sem=sems[1].at[index + h],
                device_id=(place.frame, place.tile + hops[h]),
                device_id_type=MESH,
            )
            for h in range(len(hops))
        ]

    def start(self):
        @pl.when(self.roles[0])
        def _():
            self.copies[0]().start()

    def forward(self, h=1):
        if h >= len(self.hops):
            return

        @pl.when(self.roles[h])
        def _():
            self.copies[h - 1]().wait_recv()
            self.copies[h]().start()

    def wait_recv(self):
        @pl.when(self.roles[-1])
        def _():
            self.copies[-1]().wait_recv()

    def wait_send(self):
        for h in range(len(self.hops)):

            @pl.when(self.roles[h])
            def _(h=h):
                self.copies[h]().wait_send()


class Roads:
    def __init__(self, place, sems, relay):
        self.place, self.sems, self.relay = place, sems, relay
        self.semaphores = 0
        self.blocks = 0
        self.routes = []

    def add(self, hops, source, origin, target):
        relays = [self.relay.at[self.blocks + h] for h in range(len(hops) - 1)]
        route = Route(self.place, self.sems, self.semaphores, hops, source, origin, target, relays)
        self.semaphores += len(hops)
        self.blocks += len(hops) - 1
        self.routes.append(route)
        return route

    def across(self, step, half, tall, origin, target):
        def rows_hold(row, rows):
            return row < rows - 1 if tall else row >= 0

        start, last = (4, 0) if step < 0 else (3, TILE_COLS - 1)
        hops = (-4, 3) if step < 0 else (-3, 4)
        crossing = self.add(
            hops if half == 0 else hops[::-1],
            lambda column, row, rows: both(column == start, rows_hold(row, rows)),
            origin,
            target,
        )
        straight = self.add(
            (step,),
            lambda column, row, rows: both(
                both(column != start, column != last), rows_hold(row, rows)
            ),
            origin,
            target,
        )
        return [crossing, straight]

    def along(self, step, origin, target):
        if step < 0:
            return [self.add((step,), lambda c, r, n: r > 0, origin, target)]
        return [self.add((step,), lambda c, r, n: r < n - 1, origin, target)]


def each(routes, what, *args):
    for route in routes:
        getattr(route, what)(*args)


def pieces():
    height = SIDE // PIECES
    return [(b, k * height, height) for k in range(PIECES) for b in range(2)]


def halo_kernel(
    tile_ref, meta_ref, region, metas, packed, blank, meta_blank, relay, local_sem, blank_sem,
    send_sem, recv_sem
):
    place = Place()
    roads = Roads(place, (send_sem, recv_sem), relay)
    upper, lower = pl.ds(0, SIDE), pl.ds(SIDE, SIDE)
    to_up, to_left, corners = [], [], []
    for i, (b, top, height) in enumerate(pieces()):
        mine, under = pl.ds(top, height), pl.ds(SIDE + top, height)
        to_up.append(roads.along(-8, packed.at[b, :, mine], region.at[b, :, under]))
        to_left.append(
            roads.across(-1, b, False, packed.at[b, :, mine], region.at[2 + b, :, mine])
        )
        corners.append(
            roads.across(-1, b, True, region.at[b, :, under], region.at[2 + b, :, under])
        )
    meta_right = roads.add((1,), lambda c, r, n: c < TILE_COLS - 1, meta_ref, metas.at[1])
    meta_down = roads.add((8,), lambda c, r, n: r < n - 1, meta_ref, metas.at[2])
    meta_relay = roads.add(
        (9,), lambda c, r, n: both(c < TILE_COLS - 1, r < n - 1), meta_ref, metas.at[3]
    )
    packs = [
        pltpu.make_async_copy(
            tile_ref.at[:, :, pl.ds(b * HALF, HALF)], packed.at[b], local_sem.at[3 + b]
        )
        for b in range(2)
    ]
    for copy in packs:
        copy.start()
    all_here = place.greet(roads.routes)
    assert roads.semaphores <= HALO_SEMS and roads.blocks <= HALO_BLOCKS, (
        roads.semaphores, roads.blocks
    )
    for copy in packs:
        copy.wait()

    own = [
        pltpu.make_async_copy(packed.at[b], region.at[b, :, upper], local_sem.at[b]) for b in range(2)
    ]
    own.append(pltpu.make_async_copy(meta_ref, metas.at[0], local_sem.at[2]))
    corner_there = both(place.right, place.down)
    above_there = both(place.left, place.up)
    blanks = []
    for b in range(2):
        for there, column, rows in (
            (place.right, 2 + b, upper),
            (place.down, b, lower),
            (corner_there, 2 + b, lower),
        ):
            blanks.append((there, blank, region.at[column, :, rows]))
    for i, there in enumerate((place.left, place.up, above_there)):
        blanks.append((there, meta_blank, metas.at[1 + i]))
    blanks = [
        (there, pltpu.make_async_copy(source, target, blank_sem.at[i]))
        for i, (there, source, target) in enumerate(blanks)
    ]

    all_here()
    for up, left in zip(to_up, to_left):
        each(up, "start")
        each(left, "start")
    meta_right.start()
    meta_down.start()
    meta_relay.start()
    blank[...] = jnp.zeros_like(blank)
    meta_blank[...] = jnp.zeros_like(meta_blank)
    for copy in own:
        copy.start()
    for there, copy in blanks:
        pl.when(jnp.logical_not(there))(copy.start)
    count = 2 * PIECES
    for step in range(count + LAG + LAG2):
        if step < count:
            each(to_left[step], "forward")
        if LAG <= step < count + LAG:
            each(to_up[step - LAG], "wait_recv")
            each(corners[step - LAG], "start")
        if step >= LAG + LAG2:
            each(corners[step - LAG - LAG2], "forward")
    for copy in own:
        copy.wait()
    for there, copy in blanks:
        pl.when(jnp.logical_not(there))(copy.wait)
    for group in (*to_left, *corners, [meta_right], [meta_down], [meta_relay]):
        each(group, "wait_recv")
    for group in (*to_up, *to_left, *corners, [meta_right], [meta_down], [meta_relay]):
        each(group, "wait_send")


HALO_SEMS = 60
HALO_BLOCKS = 16


def halo(tile, meta):
    V = pl.BlockSpec(memory_space=pltpu.VMEM)
    DMA = pltpu.SemaphoreType.DMA
    return pl.pallas_call(
        halo_kernel,
        out_shape=(
            jax.ShapeDtypeStruct((4, 2, 2 * SIDE, HALF), F32),
            jax.ShapeDtypeStruct((4, 8, HALF), jnp.int32),
        ),
        in_specs=[pl.BlockSpec(memory_space=pltpu.HBM), V],
        out_specs=(pl.BlockSpec(memory_space=pl.ANY), pl.BlockSpec(memory_space=pl.ANY)),
        scratch_shapes=[
            pltpu.VMEM((2, 2, SIDE, HALF), F32),
            pltpu.VMEM((2, SIDE, HALF), F32),
            pltpu.VMEM((8, HALF), jnp.int32),
            pltpu.VMEM((HALO_BLOCKS, 2, SIDE // PIECES, HALF), F32),
            DMA((5,)),
            DMA((9,)),
            DMA((HALO_SEMS,)),
            DMA((HALO_SEMS,)),
        ],
        compiler_params=pltpu.CompilerParams(
            collective_id=0, has_side_effects=True, vmem_limit_bytes=12 << 20
        ),
        name="halo",
    )(tile, meta)


def dft_blocks():
    numbers = np.arange(SIDE)
    phases = (np.outer(numbers, numbers) % SIDE) * (2.0 * math.pi / SIDE)
    cosine = np.cos(phases) / math.sqrt(SIDE)
    minus_sine = -np.sin(phases) / math.sqrt(SIDE)
    forward = np.block([[cosine, -minus_sine], [minus_sine, cosine]])
    backward = np.block([[cosine, minus_sine], [-minus_sine, cosine]])
    return jnp.asarray(forward, BF16), jnp.asarray(backward, BF16)


def fit_kernel(
    meta_ref, region_ref, probe_ref, amps_ref, fwd_ref, bwd_ref, left_ref, right_ref,
    rolled, wave, half, far,
):
    count = meta_ref[2, 0]
    pairs = (count + 1) // 2
    left_ref[...] = jnp.zeros_like(left_ref)
    right_ref[...] = jnp.zeros_like(right_ref)
    lanes = lax.broadcasted_iota(jnp.int32, (CHUNK, SIDE), 1)
    steps = SIDE // CHUNK

    def make_wave(pair):
        for k in range(2):
            slot = 2 * pair + k
            row, col = meta_ref[0, slot], meta_ref[1, slot]
            inside = lanes >= col
            for step in range(steps):
                here = pl.ds(step * CHUNK, CHUNK)
                there = pl.ds(row + step * CHUNK, CHUNK)
                probe_re = pltpu.roll(probe_ref[0, here, :], col, 1)
                probe_im = pltpu.roll(probe_ref[1, here, :], col, 1)
                rolled[k, 0, here, :] = probe_re
                rolled[k, 1, here, :] = probe_im
                part = []
                for c in range(2):
                    near = jnp.concatenate([region_ref[0, c, there, :], region_ref[1, c, there, :]], 1)
                    wide = jnp.concatenate([region_ref[2, c, there, :], region_ref[3, c, there, :]], 1)
                    part.append(jnp.where(inside, near, wide))
                cols = pl.ds(k * SIDE, SIDE)
                wave[here, cols] = (probe_re * part[0] - probe_im * part[1]).astype(BF16)
                wave[pl.ds(SIDE + step * CHUNK, CHUNK), cols] = (
                    probe_re * part[1] + probe_im * part[0]
                ).astype(BF16)

    def transform(first, second):
        for k in range(2):
            cols = pl.ds(k * SIDE, SIDE)
            for c in range(2):
                rows = pl.ds(c * SIDE, SIDE)
                half[cols, rows] = jnp.dot(
                    first[rows, :], wave[:, cols], preferred_element_type=F32
                ).astype(BF16)
        for c in range(2):
            cols = pl.ds(c * SIDE, SIDE)
            far[c] = jnp.dot(half[...], second[:, cols], preferred_element_type=F32)

    def correct(pair):
        for k in range(2):
            cols = pl.ds(k * SIDE, SIDE)
            for step in range(steps):
                here = pl.ds(step * CHUNK, CHUNK)
                there = pl.ds(k * SIDE + step * CHUNK, CHUNK)
                far_re, far_im = far[0, there, :], far[1, there, :]
                measured = amps_ref[2 * pair + k, here, :].astype(F32)
                inverse = jnp.minimum(lax.rsqrt(far_re * far_re + far_im * far_im), 2.0)
                retained = 1.0 - measured * inverse
                wave[here, cols] = (far_re * retained).astype(BF16)
                wave[pl.ds(SIDE + step * CHUNK, CHUNK), cols] = (far_im * retained).astype(BF16)

    def deposit(pair):
        for k in range(2):
            slot = 2 * pair + k
            row, col = meta_ref[0, slot], meta_ref[1, slot]
            used = slot < count
            inside = lanes >= jnp.where(used, col, 2 * SIDE)
            outside = lanes < jnp.where(used, col, 0)
            for step in range(steps):
                here = pl.ds(step * CHUNK, CHUNK)
                there = pl.ds(row + step * CHUNK, CHUNK)
                from_ = pl.ds(k * SIDE + step * CHUNK, CHUNK)
                near_re, near_im = far[0, from_, :], far[1, from_, :]
                probe_re, probe_im = rolled[k, 0, here, :], rolled[k, 1, here, :]
                grads = (
                    probe_re * near_re + probe_im * near_im,
                    probe_re * near_im - probe_im * near_re,
                )
                for c in range(2):
                    near = jnp.where(inside, grads[c], 0.0)
                    wide = jnp.where(outside, grads[c], 0.0)
                    for b in range(2):
                        cols = slice(b * HALF, (b + 1) * HALF)
                        left_ref[b, c, there, :] += near[:, cols]
                        right_ref[b, c, there, :] += wide[:, cols]

    def body(pair, carry):
        make_wave(pair)
        transform(fwd_ref, bwd_ref)
        correct(pair)
        transform(bwd_ref, fwd_ref)
        deposit(pair)
        return carry

    lax.fori_loop(0, pairs, body, 0)


def fit(meta, region, probe, amps):
    fwd, bwd = dft_blocks()
    V = pl.BlockSpec(memory_space=pltpu.VMEM)
    S = pl.BlockSpec(memory_space=pltpu.SMEM)
    shape = jax.ShapeDtypeStruct((2, 2, 2 * SIDE, HALF), F32)
    return pl.pallas_call(
        fit_kernel,
        out_shape=(shape, shape),
        in_specs=[S, V, V, V, V, V],
        out_specs=(V, V),
        scratch_shapes=[
            pltpu.VMEM((2, 2, SIDE, SIDE), F32),
            pltpu.VMEM((2 * SIDE, 2 * SIDE), BF16),
            pltpu.VMEM((2 * SIDE, 2 * SIDE), BF16),
            pltpu.VMEM((2, 2 * SIDE, SIDE), F32),
        ],
        compiler_params=pltpu.CompilerParams(vmem_limit_bytes=24 << 20),
        name="fit",
    )(meta, region, probe, amps, fwd, bwd)


def join_kernel(
    metas, tile_ref, region, left_ref, right_ref, probe_ref, out_ref,
    corner, from_left, from_up, partner_tile, weights, rims, edge_right, edge_down,
    power, lighting, flow_x, flow_y, relay, local_sem, over_send, over_recv, send_sem, recv_sem,
):
    place = Place()
    partner = (1 - place.frame, place.tile)
    roads = Roads(place, (send_sem, recv_sem), relay)
    upper, lower = pl.ds(0, SIDE), pl.ds(SIDE, SIDE)
    edges = (
        pltpu.make_async_copy(region.at[2, :, upper], edge_right, local_sem.at[0]),
        pltpu.make_async_copy(region.at[pl.ds(0, 2), :, pl.ds(SIDE, 8)], edge_down, local_sem.at[1]),
    )
    for copy in edges:
        copy.start()

    corners, merged, plain = [], [], []
    for b, top, height in pieces():
        mine, under = pl.ds(top, height), pl.ds(SIDE + top, height)
        corners.append(
            roads.across(1, b, True, right_ref.at[b, :, under], corner.at[b, :, mine])
        )
        merged.append(roads.along(TILE_COLS, corner.at[b, :, mine], from_up.at[b, :, mine]))
        plain.append(
            roads.across(1, b, False, right_ref.at[b, :, mine], from_left.at[b, :, mine])
        )
    rim_right = roads.add((1,), lambda c, r, n: c < TILE_COLS - 1, rims.at[0], rims.at[1])
    rim_down = roads.add((TILE_COLS,), lambda c, r, n: r < n - 1, rims.at[2], rims.at[3])
    assert roads.semaphores <= JOIN_SEMS and roads.blocks <= JOIN_BLOCKS
    all_here = place.greet(roads.routes, partner)
    tile_over, weight_over = (
        pltpu.make_async_remote_copy(
            src_ref=source,
            dst_ref=target,
            send_sem=over_send.at[i],
            recv_sem=over_recv.at[i],
            device_id=partner,
            device_id_type=MESH,
        )
        for i, (source, target) in enumerate(
            ((tile_ref, partner_tile), (weights.at[0], weights.at[1]))
        )
    )

    all_here()
    tile_over.start()
    for sent in (*corners, *plain):
        each(sent, "start")

    @pl.when(jnp.logical_not(place.left))
    def _():
        from_left[...] = jnp.zeros_like(from_left)
        rims[1] = jnp.zeros((8, SIDE), F32)

    @pl.when(jnp.logical_not(place.up))
    def _():
        from_up[...] = jnp.zeros_like(from_up)
        rims[3] = jnp.zeros((8, SIDE), F32)

    rims[0] = jnp.zeros((8, SIDE), F32)
    rims[2] = jnp.zeros((8, SIDE), F32)

    for copy in edges:
        copy.wait()
    tile_over.wait_recv()
    lanes = lax.broadcasted_iota(jnp.int32, (SIDE, SIDE), 1)
    rows = lax.broadcasted_iota(jnp.int32, (SIDE, SIDE), 0)
    x_lives = jnp.logical_or(lanes < SIDE - 1, place.right)
    y_lives = jnp.logical_or(rows < SIDE - 1, place.down)
    total = jnp.full((SIDE, SIDE), smoothing, F32)
    for c in range(2):
        centre = tile_ref[c]
        beyond = pltpu.roll(edge_right[c], HALF - 1, 1)
        ahead = jnp.where(
            lanes == SIDE - 1, jnp.concatenate([beyond, beyond], 1), pltpu.roll(centre, SIDE - 1, 1)
        )
        diff_x = jnp.where(x_lives, ahead - centre, 0.0)
        below = jnp.concatenate([edge_down[0, c, 0:1, :], edge_down[1, c, 0:1, :]], 1)
        ahead = jnp.where(
            rows == SIDE - 1, jnp.broadcast_to(below, (SIDE, SIDE)), pltpu.roll(centre, SIDE - 1, 0)
        )
        diff_y = jnp.where(y_lives, ahead - centre, 0.0)
        diff_t = partner_tile[c] - centre
        flow_x[c] = diff_x
        flow_y[c] = diff_y
        total = total + diff_x * diff_x + diff_y * diff_y + diff_t * diff_t
    weight = lax.rsqrt(total)
    weights[0] = weight
    weight_over.start()
    for c in range(2):
        flow = weight * flow_x[c]
        flow_x[c] = flow
        rims[0, c : c + 1, :] = flow[:, HALF:].T[HALF - 1 : HALF, :]
        flow = weight * flow_y[c]
        flow_y[c] = flow
        rims[2, c : c + 1, :] = flow[SIDE - 1 : SIDE, :]
    rim_right.start()
    rim_down.start()

    lighted = probe_ref[0] * probe_ref[0] + probe_ref[1] * probe_ref[1]
    floor = damping * jnp.max(lighted) + 1e-6
    power[...] = jnp.zeros_like(power)
    for b in range(2):
        power[b, lower, :] = lighted[:, b * HALF : (b + 1) * HALF]
    lighting[...] = jnp.zeros_like(lighting)
    chunk_lanes = lax.broadcasted_iota(jnp.int32, (CHUNK, SIDE), 1)

    def lamp(number, carry):
        source, slot = number // SLOTS, number % SLOTS
        row, col = metas[source, 0, slot], metas[source, 1, slot]
        used = slot < metas[source, 2, 0]
        beside = source % 2 == 1
        start = SIDE + SIDE * (source // 2) - row
        low = jnp.where(beside, 0, jnp.where(used, col, 2 * SIDE))
        high = jnp.where(beside, jnp.where(used, col, 0), 2 * SIDE)
        lit = both(chunk_lanes >= low, chunk_lanes < high)
        for step in range(SIDE // CHUNK):
            here = pl.ds(step * CHUNK, CHUNK)
            there = pl.ds(start + step * CHUNK, CHUNK)
            light = jnp.concatenate([power[0, there, :], power[1, there, :]], 1)
            lighting[here, :] += jnp.where(lit, pltpu.roll(light, col, 1), 0.0)
        return carry

    count = 2 * PIECES
    for step in range(count + LAG):
        if step < count:
            each(corners[step], "forward")
        if step >= LAG:
            number = step - LAG
            b, top, height = pieces()[number]
            mine = pl.ds(top, height)
            each(corners[number], "wait_recv")

            @pl.when(both(place.down, place.left))
            def _():
                corner[b, :, mine] += left_ref[b, :, pl.ds(SIDE + top, height)]

            @pl.when(both(place.down, jnp.logical_not(place.left)))
            def _():
                corner[b, :, mine] = left_ref[b, :, pl.ds(SIDE + top, height)]

            each(merged[number], "start")
    for step in range(count):
        lamps = 4 * SLOTS // count
        lax.fori_loop(step * lamps, (step + 1) * lamps, lamp, 0)
        each(plain[step], "forward")

    weight_over.wait_recv()
    for sent in ([rim_right], [rim_down], *plain, *merged):
        each(sent, "wait_recv")
    for c in range(2):
        centre = tile_ref[c]
        diff_t = partner_tile[c] - centre
        rim = jnp.broadcast_to(rims[1, c : c + 1, :], (HALF, SIDE)).T
        rim = jnp.concatenate([rim, rim], 1)
        flow = flow_x[c]
        grad = jnp.where(lanes == 0, rim, pltpu.roll(flow, 1, 1)) - flow
        rim = jnp.broadcast_to(rims[3, c : c + 1, :], (SIDE, SIDE))
        flow = flow_y[c]
        grad = grad + jnp.where(rows == 0, rim, pltpu.roll(flow, 1, 0)) - flow
        grad = grad - (weights[0] + weights[1]) * diff_t
        fit = jnp.concatenate(
            [left_ref[b, c, upper, :] + from_left[b, c] + from_up[b, c] for b in range(2)], 1
        )
        out_ref[c] = centre - fit / (lighting[...] + floor) - variation_weight * grad
    tile_over.wait_send()
    weight_over.wait_send()
    for sent in ([rim_right], [rim_down], *corners, *plain, *merged):
        each(sent, "wait_send")


JOIN_SEMS = 60
JOIN_BLOCKS = 16
SLOTS = 16


def join(metas, tile, region, left, right, probe):
    V = pl.BlockSpec(memory_space=pltpu.VMEM)
    S = pl.BlockSpec(memory_space=pltpu.SMEM)
    block = (2, SIDE, HALF)
    return pl.pallas_call(
        join_kernel,
        out_shape=jax.ShapeDtypeStruct((2, SIDE, SIDE), F32),
        in_specs=[S, V, pl.BlockSpec(memory_space=pl.ANY), V, V, V],
        out_specs=V,
        scratch_shapes=[
            pltpu.VMEM((2, *block), F32),
            pltpu.VMEM((2, *block), F32),
            pltpu.VMEM((2, *block), F32),
            pltpu.VMEM((2, SIDE, SIDE), F32),
            pltpu.VMEM((2, SIDE, SIDE), F32),
            pltpu.VMEM((4, 8, SIDE), F32),
            pltpu.VMEM(block, F32),
            pltpu.VMEM((2, 2, 8, HALF), F32),
            pltpu.VMEM((2, 3 * SIDE, HALF), F32),
            pltpu.VMEM((SIDE, SIDE), F32),
            pltpu.VMEM((2, SIDE, SIDE), F32),
            pltpu.VMEM((2, SIDE, SIDE), F32),
            pltpu.VMEM((JOIN_BLOCKS, 2, SIDE // PIECES, HALF), F32),
            pltpu.SemaphoreType.DMA((2,)),
            pltpu.SemaphoreType.DMA((2,)),
            pltpu.SemaphoreType.DMA((2,)),
            pltpu.SemaphoreType.DMA((JOIN_SEMS,)),
            pltpu.SemaphoreType.DMA((JOIN_SEMS,)),
        ],
        compiler_params=pltpu.CompilerParams(
            collective_id=1, has_side_effects=True, vmem_limit_bytes=20 << 20
        ),
        name="join",
    )(metas, tile, region, left, right, probe)


def local(object_tiles, probe_field, amplitudes, offsets, counts):
    tile = object_tiles[0, 0]
    slots = amplitudes.shape[1]
    meta = jnp.concatenate([offsets[0].T, jnp.broadcast_to(counts, (6, slots))], 0)
    meta = jnp.pad(meta, ((0, 0), (0, HALF - slots)))
    region, metas = halo(tile, meta)
    left, right = fit(meta, region, probe_field, amplitudes[0])
    return join(metas, tile, region, left, right, probe_field)[None, None]


def solution(mesh):
    return jax.shard_map(
        local,
        mesh=mesh,
        in_specs=(
            P("frame", "tile", None, None, None),
            P(),
            P("frame", "tile", None, None),
            P("frame", "tile", None),
            P("frame", "tile"),
        ),
        out_specs=P("frame", "tile", None, None, None),
        check_vma=False,
    )
```

```python
import functools
import math

import jax
import jax.numpy as jnp
import numpy as np
from jax import lax
from jax.experimental import pallas as pl
from jax.experimental.pallas import tpu as pltpu
from jax.sharding import PartitionSpec as P

TILE_COLS = 8
SIDE = 256
HALF = 128
CHUNK = 32
PIECES = 4
LAG = 3
LAG2 = 2
F32, BF16 = jnp.float32, jnp.bfloat16
MESH = pl.DeviceIdType.MESH

damping = 0.1
variation_weight = 0.2
smoothing = 0.25


def both(a, b):
    return jnp.logical_and(a, b)


class Place:
    def __init__(self):
        self.frame = lax.axis_index("frame")
        self.tile = lax.axis_index("tile")
        self.tiles = lax.axis_size("tile")
        column, row = self.tile % TILE_COLS, self.tile // TILE_COLS
        self.left = column > 0
        self.right = column < TILE_COLS - 1
        self.up = row > 0
        self.down = row < self.tiles // TILE_COLS - 1

    def holds(self, source, step):
        tile = self.tile - step
        there = both(tile >= 0, tile < self.tiles)
        return both(there, source(tile % TILE_COLS, tile // TILE_COLS, self.tiles // TILE_COLS))

    def greet(self, routes, partner=None):
        barrier = pltpu.get_barrier_semaphore()
        before, after = {}, {}
        for route in routes:
            for h, step in enumerate(route.hops):
                for known, role in ((after, route.roles[h]), (before, route.roles[h + 1])):
                    known[step] = jnp.logical_or(known[step], role) if step in known else role
        for step, there in before.items():

            @pl.when(there)
            def _(step=step):
                device = (self.frame, self.tile - step)
                pl.semaphore_signal(barrier, inc=1, device_id=device, device_id_type=MESH)

        total = jnp.int32(0)
        for there in after.values():
            total = total + there.astype(jnp.int32)
        if partner is not None:
            total = total + 1
            pl.semaphore_signal(barrier, inc=1, device_id=partner, device_id_type=MESH)
        return lambda: pl.semaphore_wait(barrier, total)


class Route:
    def __init__(self, place, sems, index, hops, source, origin, target, relays=()):
        assert len(relays) == len(hops) - 1
        steps = [sum(hops[:h]) for h in range(len(hops) + 1)]
        self.hops = hops
        self.roles = [place.holds(source, step) for step in steps]
        stops = [origin, *relays, target]
        self.copies = [
            functools.partial(
                pltpu.make_async_remote_copy,
                src_ref=stops[h],
                dst_ref=stops[h + 1],
                send_sem=sems[0].at[index + h],
                recv_sem=sems[1].at[index + h],
                device_id=(place.frame, place.tile + hops[h]),
                device_id_type=MESH,
            )
            for h in range(len(hops))
        ]

    def start(self):
        @pl.when(self.roles[0])
        def _():
            self.copies[0]().start()

    def forward(self, h=1):
        if h >= len(self.hops):
            return

        @pl.when(self.roles[h])
        def _():
            self.copies[h - 1]().wait_recv()
            self.copies[h]().start()

    def wait_recv(self):
        @pl.when(self.roles[-1])
        def _():
            self.copies[-1]().wait_recv()

    def wait_send(self):
        for h in range(len(self.hops)):

            @pl.when(self.roles[h])
            def _(h=h):
                self.copies[h]().wait_send()


class Roads:
    def __init__(self, place, sems, relay):
        self.place, self.sems, self.relay = place, sems, relay
        self.semaphores = 0
        self.blocks = 0
        self.routes = []

    def add(self, hops, source, origin, target):
        relays = [self.relay.at[self.blocks + h] for h in range(len(hops) - 1)]
        route = Route(self.place, self.sems, self.semaphores, hops, source, origin, target, relays)
        self.semaphores += len(hops)
        self.blocks += len(hops) - 1
        self.routes.append(route)
        return route

    def across(self, step, half, tall, origin, target):
        def rows_hold(row, rows):
            return row < rows - 1 if tall else row >= 0

        start, last = (4, 0) if step < 0 else (3, TILE_COLS - 1)
        hops = (-4, 3) if step < 0 else (-3, 4)
        crossing = self.add(
            hops if half == 0 else hops[::-1],
            lambda column, row, rows: both(column == start, rows_hold(row, rows)),
            origin,
            target,
        )
        straight = self.add(
            (step,),
            lambda column, row, rows: both(
                both(column != start, column != last), rows_hold(row, rows)
            ),
            origin,
            target,
        )
        return [crossing, straight]

    def along(self, step, origin, target):
        if step < 0:
            return [self.add((step,), lambda c, r, n: r > 0, origin, target)]
        return [self.add((step,), lambda c, r, n: r < n - 1, origin, target)]


def each(routes, what, *args):
    for route in routes:
        getattr(route, what)(*args)


def pieces():
    height = SIDE // PIECES
    return [(b, k * height, height) for k in range(PIECES) for b in range(2)]


def halo_kernel(
    tile_ref, meta_ref, amps_ref, probe_ref, table_ref, region, metas, amps_out, probe_out, table_out, packed, blank, meta_blank, relay, local_sem, blank_sem,
    send_sem, recv_sem
):
    place = Place()
    roads = Roads(place, (send_sem, recv_sem), relay)
    upper, lower = pl.ds(0, SIDE), pl.ds(SIDE, SIDE)
    to_up, to_left, corners = [], [], []
    for i, (b, top, height) in enumerate(pieces()):
        mine, under = pl.ds(top, height), pl.ds(SIDE + top, height)
        to_up.append(roads.along(-8, packed.at[b, :, mine], region.at[b, :, under]))
        to_left.append(
            roads.across(-1, b, False, packed.at[b, :, mine], region.at[2 + b, :, mine])
        )
        corners.append(
            roads.across(-1, b, True, region.at[b, :, under], region.at[2 + b, :, under])
        )
    meta_right = roads.add((1,), lambda c, r, n: c < TILE_COLS - 1, meta_ref, metas.at[1])
    meta_down = roads.add((8,), lambda c, r, n: r < n - 1, meta_ref, metas.at[2])
    meta_relay = roads.add(
        (9,), lambda c, r, n: both(c < TILE_COLS - 1, r < n - 1), meta_ref, metas.at[3]
    )
    packs = [
        pltpu.make_async_copy(
            tile_ref.at[:, :, pl.ds(b * HALF, HALF)], packed.at[b], local_sem.at[3 + b]
        )
        for b in range(2)
    ]
    for copy in packs:
        copy.start()
    all_here = place.greet(roads.routes)
    assert roads.semaphores <= HALO_SEMS and roads.blocks <= HALO_BLOCKS, (
        roads.semaphores, roads.blocks
    )
    for copy in packs:
        copy.wait()

    own = [
        pltpu.make_async_copy(packed.at[b], region.at[b, :, upper], local_sem.at[b]) for b in range(2)
    ]
    own.append(pltpu.make_async_copy(meta_ref, metas.at[0], local_sem.at[2]))
    for i, (source, target) in enumerate(
        ((amps_ref, amps_out), (probe_ref, probe_out), (table_ref, table_out))
    ):
        own.append(pltpu.make_async_copy(source, target, local_sem.at[5 + i]))
    corner_there = both(place.right, place.down)
    above_there = both(place.left, place.up)
    blanks = []
    for b in range(2):
        for there, column, rows in (
            (place.right, 2 + b, upper),
            (place.down, b, lower),
            (corner_there, 2 + b, lower),
        ):
            blanks.append((there, blank, region.at[column, :, rows]))
    for i, there in enumerate((place.left, place.up, above_there)):
        blanks.append((there, meta_blank, metas.at[1 + i]))
    blanks = [
        (there, pltpu.make_async_copy(source, target, blank_sem.at[i]))
        for i, (there, source, target) in enumerate(blanks)
    ]

    all_here()
    for up, left in zip(to_up, to_left):
        each(up, "start")
        each(left, "start")
    meta_right.start()
    meta_down.start()
    meta_relay.start()
    blank[...] = jnp.zeros_like(blank)
    meta_blank[...] = jnp.zeros_like(meta_blank)
    for copy in own:
        copy.start()
    for there, copy in blanks:
        pl.when(jnp.logical_not(there))(copy.start)
    count = 2 * PIECES
    for step in range(count + LAG + LAG2):
        if step < count:
            each(to_left[step], "forward")
        if LAG <= step < count + LAG:
            each(to_up[step - LAG], "wait_recv")
            each(corners[step - LAG], "start")
        if step >= LAG + LAG2:
            each(corners[step - LAG - LAG2], "forward")
    for copy in own:
        copy.wait()
    for there, copy in blanks:
        pl.when(jnp.logical_not(there))(copy.wait)
    for group in (*to_left, *corners, [meta_right], [meta_down], [meta_relay]):
        each(group, "wait_recv")
    for group in (*to_up, *to_left, *corners, [meta_right], [meta_down], [meta_relay]):
        each(group, "wait_send")


HALO_SEMS = 60
HALO_BLOCKS = 16


def in_hbm(array):
    return pltpu.with_memory_space_constraint(array, pltpu.HBM)


def halo(tile, meta, amps, probe):
    V = pl.BlockSpec(memory_space=pltpu.VMEM)
    A = pl.BlockSpec(memory_space=pl.ANY)
    DMA = pltpu.SemaphoreType.DMA
    return pl.pallas_call(
        halo_kernel,
        out_shape=(
            jax.ShapeDtypeStruct((4, 2, 2 * SIDE, HALF), F32),
            jax.ShapeDtypeStruct((4, 8, HALF), jnp.int32),
            jax.ShapeDtypeStruct(amps.shape, BF16),
            jax.ShapeDtypeStruct(probe.shape, F32),
            jax.ShapeDtypeStruct((2, SIDE, SIDE), BF16),
        ),
        in_specs=[A, V, A, A, A],
        out_specs=(A, A, A, A, A),
        scratch_shapes=[
            pltpu.VMEM((2, 2, SIDE, HALF), F32),
            pltpu.VMEM((2, SIDE, HALF), F32),
            pltpu.VMEM((8, HALF), jnp.int32),
            pltpu.VMEM((HALO_BLOCKS, 2, SIDE // PIECES, HALF), F32),
            DMA((8,)),
            DMA((9,)),
            DMA((HALO_SEMS,)),
            DMA((HALO_SEMS,)),
        ],
        compiler_params=pltpu.CompilerParams(
            collective_id=0, has_side_effects=True, vmem_limit_bytes=12 << 20
        ),
        name="halo",
    )(in_hbm(tile), meta, in_hbm(amps), in_hbm(probe), in_hbm(dft_table()))


def dft_table():
    numbers = np.arange(SIDE)
    phases = (np.outer(numbers, numbers) % SIDE) * (2.0 * math.pi / SIDE)
    cosine = np.cos(phases) / math.sqrt(SIDE)
    minus_sine = -np.sin(phases) / math.sqrt(SIDE)
    return jnp.asarray(np.stack([cosine, minus_sine]), BF16)


def fit_kernel(
    meta_ref, region_ref, probe_ref, amps_ref, table, left_ref, right_ref,
    fwd_ref, bwd_ref, rolled, wave, half, far,
):
    count = meta_ref[2, 0]
    pairs = (count + 1) // 2
    left_ref[...] = jnp.zeros_like(left_ref)
    right_ref[...] = jnp.zeros_like(right_ref)
    lanes = lax.broadcasted_iota(jnp.int32, (CHUNK, SIDE), 1)
    steps = SIDE // CHUNK

    def make_wave(pair):
        for k in range(2):
            slot = 2 * pair + k
            row, col = meta_ref[0, slot], meta_ref[1, slot]
            inside = lanes >= col
            for step in range(steps):
                here = pl.ds(step * CHUNK, CHUNK)
                there = pl.ds(row + step * CHUNK, CHUNK)
                probe_re = pltpu.roll(probe_ref[0, here, :], col, 1)
                probe_im = pltpu.roll(probe_ref[1, here, :], col, 1)
                rolled[k, 0, here, :] = probe_re
                rolled[k, 1, here, :] = probe_im
                part = []
                for c in range(2):
                    near = jnp.concatenate([region_ref[0, c, there, :], region_ref[1, c, there, :]], 1)
                    wide = jnp.concatenate([region_ref[2, c, there, :], region_ref[3, c, there, :]], 1)
                    part.append(jnp.where(inside, near, wide))
                cols = pl.ds(k * SIDE, SIDE)
                wave[here, cols] = (probe_re * part[0] - probe_im * part[1]).astype(BF16)
                wave[pl.ds(SIDE + step * CHUNK, CHUNK), cols] = (
                    probe_re * part[1] + probe_im * part[0]
                ).astype(BF16)

    def transform(first, second):
        for k in range(2):
            cols = pl.ds(k * SIDE, SIDE)
            for c in range(2):
                rows = pl.ds(c * SIDE, SIDE)
                half[cols, rows] = jnp.dot(
                    first[rows, :], wave[:, cols], preferred_element_type=F32
                ).astype(BF16)
        for k in range(2):
            rows = pl.ds(k * SIDE, SIDE)
            got = jnp.dot(half[rows, :], second[...], preferred_element_type=F32)
            far[0, rows, :] = got[:, :SIDE]
            far[1, rows, :] = got[:, SIDE:]

    def correct(pair):
        for k in range(2):
            cols = pl.ds(k * SIDE, SIDE)
            for step in range(steps):
                here = pl.ds(step * CHUNK, CHUNK)
                there = pl.ds(k * SIDE + step * CHUNK, CHUNK)
                far_re, far_im = far[0, there, :], far[1, there, :]
                measured = amps_ref[2 * pair + k, here, :].astype(F32)
                inverse = jnp.minimum(lax.rsqrt(far_re * far_re + far_im * far_im), 2.0)
                retained = 1.0 - measured * inverse
                wave[here, cols] = (far_re * retained).astype(BF16)
                wave[pl.ds(SIDE + step * CHUNK, CHUNK), cols] = (far_im * retained).astype(BF16)

    def deposit(pair):
        for k in range(2):
            slot = 2 * pair + k
            row, col = meta_ref[0, slot], meta_ref[1, slot]
            used = slot < count
            inside = lanes >= jnp.where(used, col, 2 * SIDE)
            outside = lanes < jnp.where(used, col, 0)
            for step in range(steps):
                here = pl.ds(step * CHUNK, CHUNK)
                there = pl.ds(row + step * CHUNK, CHUNK)
                from_ = pl.ds(k * SIDE + step * CHUNK, CHUNK)
                near_re, near_im = far[0, from_, :], far[1, from_, :]
                probe_re, probe_im = rolled[k, 0, here, :], rolled[k, 1, here, :]
                grads = (
                    probe_re * near_re + probe_im * near_im,
                    probe_re * near_im - probe_im * near_re,
                )
                for c in range(2):
                    near = jnp.where(inside, grads[c], 0.0)
                    wide = jnp.where(outside, grads[c], 0.0)
                    for b in range(2):
                        cols = slice(b * HALF, (b + 1) * HALF)
                        left_ref[b, c, there, :] += near[:, cols]
                        right_ref[b, c, there, :] += wide[:, cols]

    near, far_side = pl.ds(0, SIDE), pl.ds(SIDE, SIDE)
    for block in (near, far_side):
        fwd_ref[block, block] = table[0]
        bwd_ref[block, block] = table[0]
    fwd_ref[near, far_side] = -table[1]
    fwd_ref[far_side, near] = table[1]
    bwd_ref[near, far_side] = table[1]
    bwd_ref[far_side, near] = -table[1]

    def body(pair, carry):
        make_wave(pair)
        transform(fwd_ref, bwd_ref)
        correct(pair)
        transform(bwd_ref, fwd_ref)
        deposit(pair)
        return carry

    lax.fori_loop(0, pairs, body, 0)


def fit(meta, region, probe, amps, table):
    V = pl.BlockSpec(memory_space=pltpu.VMEM)
    S = pl.BlockSpec(memory_space=pltpu.SMEM)
    shape = jax.ShapeDtypeStruct((2, 2, 2 * SIDE, HALF), F32)
    return pl.pallas_call(
        fit_kernel,
        out_shape=(shape, shape),
        in_specs=[S, V, V, V, V],
        out_specs=(V, V),
        scratch_shapes=[
            pltpu.VMEM((2 * SIDE, 2 * SIDE), BF16),
            pltpu.VMEM((2 * SIDE, 2 * SIDE), BF16),
            pltpu.VMEM((2, 2, SIDE, SIDE), F32),
            pltpu.VMEM((2 * SIDE, 2 * SIDE), BF16),
            pltpu.VMEM((2 * SIDE, 2 * SIDE), BF16),
            pltpu.VMEM((2, 2 * SIDE, SIDE), F32),
        ],
        compiler_params=pltpu.CompilerParams(vmem_limit_bytes=24 << 20),
        name="fit",
    )(meta, region, probe, amps, table)


def join_kernel(
    metas, tile_ref, region, left_ref, right_ref, probe_ref, out_ref,
    corner, from_left, from_up, partner_tile, weights, rims, edge_right, edge_down,
    power, lighting, flow_x, flow_y, relay, local_sem, over_send, over_recv, send_sem, recv_sem,
):
    place = Place()
    partner = (1 - place.frame, place.tile)
    roads = Roads(place, (send_sem, recv_sem), relay)
    upper, lower = pl.ds(0, SIDE), pl.ds(SIDE, SIDE)
    edges = (
        pltpu.make_async_copy(region.at[2, :, upper], edge_right, local_sem.at[0]),
        pltpu.make_async_copy(region.at[pl.ds(0, 2), :, pl.ds(SIDE, 8)], edge_down, local_sem.at[1]),
    )
    for copy in edges:
        copy.start()

    corners, merged, plain = [], [], []
    for b, top, height in pieces():
        mine, under = pl.ds(top, height), pl.ds(SIDE + top, height)
        corners.append(
            roads.across(1, b, True, right_ref.at[b, :, under], corner.at[b, :, mine])
        )
        merged.append(roads.along(TILE_COLS, corner.at[b, :, mine], from_up.at[b, :, mine]))
        plain.append(
            roads.across(1, b, False, right_ref.at[b, :, mine], from_left.at[b, :, mine])
        )
    rim_right = roads.add((1,), lambda c, r, n: c < TILE_COLS - 1, rims.at[0], rims.at[1])
    rim_down = roads.add((TILE_COLS,), lambda c, r, n: r < n - 1, rims.at[2], rims.at[3])
    assert roads.semaphores <= JOIN_SEMS and roads.blocks <= JOIN_BLOCKS
    all_here = place.greet(roads.routes, partner)
    tile_over, weight_over = (
        pltpu.make_async_remote_copy(
            src_ref=source,
            dst_ref=target,
            send_sem=over_send.at[i],
            recv_sem=over_recv.at[i],
            device_id=partner,
            device_id_type=MESH,
        )
        for i, (source, target) in enumerate(
            ((tile_ref, partner_tile), (weights.at[0], weights.at[1]))
        )
    )

    all_here()
    tile_over.start()
    for sent in (*corners, *plain):
        each(sent, "start")

    @pl.when(jnp.logical_not(place.left))
    def _():
        from_left[...] = jnp.zeros_like(from_left)
        rims[1] = jnp.zeros((8, SIDE), F32)

    @pl.when(jnp.logical_not(place.up))
    def _():
        from_up[...] = jnp.zeros_like(from_up)
        rims[3] = jnp.zeros((8, SIDE), F32)

    rims[0] = jnp.zeros((8, SIDE), F32)
    rims[2] = jnp.zeros((8, SIDE), F32)

    for copy in edges:
        copy.wait()
    tile_over.wait_recv()
    lanes = lax.broadcasted_iota(jnp.int32, (SIDE, SIDE), 1)
    rows = lax.broadcasted_iota(jnp.int32, (SIDE, SIDE), 0)
    x_lives = jnp.logical_or(lanes < SIDE - 1, place.right)
    y_lives = jnp.logical_or(rows < SIDE - 1, place.down)
    total = jnp.full((SIDE, SIDE), smoothing, F32)
    for c in range(2):
        centre = tile_ref[c]
        beyond = pltpu.roll(edge_right[c], HALF - 1, 1)
        ahead = jnp.where(
            lanes == SIDE - 1, jnp.concatenate([beyond, beyond], 1), pltpu.roll(centre, SIDE - 1, 1)
        )
        diff_x = jnp.where(x_lives, ahead - centre, 0.0)
        below = jnp.concatenate([edge_down[0, c, 0:1, :], edge_down[1, c, 0:1, :]], 1)
        ahead = jnp.where(
            rows == SIDE - 1, jnp.broadcast_to(below, (SIDE, SIDE)), pltpu.roll(centre, SIDE - 1, 0)
        )
        diff_y = jnp.where(y_lives, ahead - centre, 0.0)
        diff_t = partner_tile[c] - centre
        flow_x[c] = diff_x
        flow_y[c] = diff_y
        total = total + diff_x * diff_x + diff_y * diff_y + diff_t * diff_t
    weight = lax.rsqrt(total)
    weights[0] = weight
    weight_over.start()
    for c in range(2):
        flow = weight * flow_x[c]
        flow_x[c] = flow
        rims[0, c : c + 1, :] = flow[:, HALF:].T[HALF - 1 : HALF, :]
        flow = weight * flow_y[c]
        flow_y[c] = flow
        rims[2, c : c + 1, :] = flow[SIDE - 1 : SIDE, :]
    rim_right.start()
    rim_down.start()

    lighted = probe_ref[0] * probe_ref[0] + probe_ref[1] * probe_ref[1]
    floor = damping * jnp.max(lighted) + 1e-6
    power[...] = jnp.zeros_like(power)
    for b in range(2):
        power[b, lower, :] = lighted[:, b * HALF : (b + 1) * HALF]
    lighting[...] = jnp.zeros_like(lighting)
    chunk_lanes = lax.broadcasted_iota(jnp.int32, (CHUNK, SIDE), 1)

    def lamp(number, carry):
        source, slot = number // SLOTS, number % SLOTS
        row, col = metas[source, 0, slot], metas[source, 1, slot]
        used = slot < metas[source, 2, 0]
        beside = source % 2 == 1
        start = SIDE + SIDE * (source // 2) - row
        low = jnp.where(beside, 0, jnp.where(used, col, 2 * SIDE))
        high = jnp.where(beside, jnp.where(used, col, 0), 2 * SIDE)
        lit = both(chunk_lanes >= low, chunk_lanes < high)
        for step in range(SIDE // CHUNK):
            here = pl.ds(step * CHUNK, CHUNK)
            there = pl.ds(start + step * CHUNK, CHUNK)
            light = jnp.concatenate([power[0, there, :], power[1, there, :]], 1)
            lighting[here, :] += jnp.where(lit, pltpu.roll(light, col, 1), 0.0)
        return carry

    count = 2 * PIECES
    for step in range(count + LAG):
        if step < count:
            each(corners[step], "forward")
        if step >= LAG:
            number = step - LAG
            b, top, height = pieces()[number]
            mine = pl.ds(top, height)
            each(corners[number], "wait_recv")

            @pl.when(both(place.down, place.left))
            def _():
                corner[b, :, mine] += left_ref[b, :, pl.ds(SIDE + top, height)]

            @pl.when(both(place.down, jnp.logical_not(place.left)))
            def _():
                corner[b, :, mine] = left_ref[b, :, pl.ds(SIDE + top, height)]

            each(merged[number], "start")
    for step in range(count):
        lamps = 4 * SLOTS // count
        lax.fori_loop(step * lamps, (step + 1) * lamps, lamp, 0)
        each(plain[step], "forward")

    weight_over.wait_recv()
    for sent in ([rim_right], [rim_down], *plain, *merged):
        each(sent, "wait_recv")
    for c in range(2):
        centre = tile_ref[c]
        diff_t = partner_tile[c] - centre
        rim = jnp.broadcast_to(rims[1, c : c + 1, :], (HALF, SIDE)).T
        rim = jnp.concatenate([rim, rim], 1)
        flow = flow_x[c]
        grad = jnp.where(lanes == 0, rim, pltpu.roll(flow, 1, 1)) - flow
        rim = jnp.broadcast_to(rims[3, c : c + 1, :], (SIDE, SIDE))
        flow = flow_y[c]
        grad = grad + jnp.where(rows == 0, rim, pltpu.roll(flow, 1, 0)) - flow
        grad = grad - (weights[0] + weights[1]) * diff_t
        fit = jnp.concatenate(
            [left_ref[b, c, upper, :] + from_left[b, c] + from_up[b, c] for b in range(2)], 1
        )
        out_ref[c] = centre - fit / (lighting[...] + floor) - variation_weight * grad
    tile_over.wait_send()
    weight_over.wait_send()
    for sent in ([rim_right], [rim_down], *corners, *plain, *merged):
        each(sent, "wait_send")


JOIN_SEMS = 60
JOIN_BLOCKS = 16
SLOTS = 16


def join(metas, tile, region, left, right, probe):
    V = pl.BlockSpec(memory_space=pltpu.VMEM)
    S = pl.BlockSpec(memory_space=pltpu.SMEM)
    block = (2, SIDE, HALF)
    return pl.pallas_call(
        join_kernel,
        out_shape=jax.ShapeDtypeStruct((2, SIDE, SIDE), F32),
        in_specs=[S, V, pl.BlockSpec(memory_space=pl.ANY), V, V, V],
        out_specs=V,
        scratch_shapes=[
            pltpu.VMEM((2, *block), F32),
            pltpu.VMEM((2, *block), F32),
            pltpu.VMEM((2, *block), F32),
            pltpu.VMEM((2, SIDE, SIDE), F32),
            pltpu.VMEM((2, SIDE, SIDE), F32),
            pltpu.VMEM((4, 8, SIDE), F32),
            pltpu.VMEM(block, F32),
            pltpu.VMEM((2, 2, 8, HALF), F32),
            pltpu.VMEM((2, 3 * SIDE, HALF), F32),
            pltpu.VMEM((SIDE, SIDE), F32),
            pltpu.VMEM((2, SIDE, SIDE), F32),
            pltpu.VMEM((2, SIDE, SIDE), F32),
            pltpu.VMEM((JOIN_BLOCKS, 2, SIDE // PIECES, HALF), F32),
            pltpu.SemaphoreType.DMA((2,)),
            pltpu.SemaphoreType.DMA((2,)),
            pltpu.SemaphoreType.DMA((2,)),
            pltpu.SemaphoreType.DMA((JOIN_SEMS,)),
            pltpu.SemaphoreType.DMA((JOIN_SEMS,)),
        ],
        compiler_params=pltpu.CompilerParams(
            collective_id=1, has_side_effects=True, vmem_limit_bytes=20 << 20
        ),
        name="join",
    )(metas, tile, region, left, right, probe)


def local(object_tiles, probe_field, amplitudes, offsets, counts):
    tile = object_tiles[0, 0]
    slots = amplitudes.shape[1]
    meta = jnp.concatenate([offsets[0].T, jnp.broadcast_to(counts, (6, slots))], 0)
    meta = jnp.pad(meta, ((0, 0), (0, HALF - slots)))
    region, metas, amps, probe, table = halo(tile, meta, amplitudes[0], probe_field)
    left, right = fit(meta, region, probe, amps, table)
    return join(metas, tile, region, left, right, probe)[None, None]


def solution(mesh):
    return jax.shard_map(
        local,
        mesh=mesh,
        in_specs=(
            P("frame", "tile", None, None, None),
            P(),
            P("frame", "tile", None, None),
            P("frame", "tile", None),
            P("frame", "tile"),
        ),
        out_specs=P("frame", "tile", None, None, None),
        check_vma=False,
    )
```

```python
import functools
import math

import jax
import jax.numpy as jnp
import numpy as np
from jax import lax
from jax.experimental import pallas as pl
from jax.experimental.pallas import tpu as pltpu
from jax.sharding import PartitionSpec as P

TILE_COLS = 8
SIDE = 256
HALF = 128
CHUNK = 32
GROUP = 4
PIECES = 4
LAG = 3
LAG2 = 2
F32, BF16 = jnp.float32, jnp.bfloat16
MESH = pl.DeviceIdType.MESH

damping = 0.1
variation_weight = 0.2
smoothing = 0.25


def both(a, b):
    return jnp.logical_and(a, b)


class Place:
    def __init__(self):
        self.frame = lax.axis_index("frame")
        self.tile = lax.axis_index("tile")
        self.tiles = lax.axis_size("tile")
        column, row = self.tile % TILE_COLS, self.tile // TILE_COLS
        self.left = column > 0
        self.right = column < TILE_COLS - 1
        self.up = row > 0
        self.down = row < self.tiles // TILE_COLS - 1

    def holds(self, source, step):
        tile = self.tile - step
        there = both(tile >= 0, tile < self.tiles)
        return both(there, source(tile % TILE_COLS, tile // TILE_COLS, self.tiles // TILE_COLS))

    def greet(self, routes, partner=None):
        barrier = pltpu.get_barrier_semaphore()
        before, after = {}, {}
        for route in routes:
            for h, step in enumerate(route.hops):
                for known, role in ((after, route.roles[h]), (before, route.roles[h + 1])):
                    known[step] = jnp.logical_or(known[step], role) if step in known else role
        for step, there in before.items():

            @pl.when(there)
            def _(step=step):
                device = (self.frame, self.tile - step)
                pl.semaphore_signal(barrier, inc=1, device_id=device, device_id_type=MESH)

        total = jnp.int32(0)
        for there in after.values():
            total = total + there.astype(jnp.int32)
        if partner is not None:
            total = total + 1
            pl.semaphore_signal(barrier, inc=1, device_id=partner, device_id_type=MESH)
        return lambda: pl.semaphore_wait(barrier, total)


class Route:
    def __init__(self, place, sems, index, hops, source, origin, target, relays=()):
        assert len(relays) == len(hops) - 1
        steps = [sum(hops[:h]) for h in range(len(hops) + 1)]
        self.hops = hops
        self.roles = [place.holds(source, step) for step in steps]
        stops = [origin, *relays, target]
        self.copies = [
            functools.partial(
                pltpu.make_async_remote_copy,
                src_ref=stops[h],
                dst_ref=stops[h + 1],
                send_sem=sems[0].at[index + h],
                recv_sem=sems[1].at[index + h],
                device_id=(place.frame, place.tile + hops[h]),
                device_id_type=MESH,
            )
            for h in range(len(hops))
        ]

    def start(self):
        @pl.when(self.roles[0])
        def _():
            self.copies[0]().start()

    def forward(self, h=1):
        if h >= len(self.hops):
            return

        @pl.when(self.roles[h])
        def _():
            self.copies[h - 1]().wait_recv()
            self.copies[h]().start()

    def wait_recv(self):
        @pl.when(self.roles[-1])
        def _():
            self.copies[-1]().wait_recv()

    def wait_send(self):
        for h in range(len(self.hops)):

            @pl.when(self.roles[h])
            def _(h=h):
                self.copies[h]().wait_send()


class Roads:
    def __init__(self, place, sems, relay):
        self.place, self.sems, self.relay = place, sems, relay
        self.semaphores = 0
        self.blocks = 0
        self.routes = []

    def add(self, hops, source, origin, target):
        relays = [self.relay.at[self.blocks + h] for h in range(len(hops) - 1)]
        route = Route(self.place, self.sems, self.semaphores, hops, source, origin, target, relays)
        self.semaphores += len(hops)
        self.blocks += len(hops) - 1
        self.routes.append(route)
        return route

    def across(self, step, half, tall, origin, target):
        def rows_hold(row, rows):
            return row < rows - 1 if tall else row >= 0

        start, last = (4, 0) if step < 0 else (3, TILE_COLS - 1)
        hops = (-4, 3) if step < 0 else (-3, 4)
        crossing = self.add(
            hops if half == 0 else hops[::-1],
            lambda column, row, rows: both(column == start, rows_hold(row, rows)),
            origin,
            target,
        )
        straight = self.add(
            (step,),
            lambda column, row, rows: both(
                both(column != start, column != last), rows_hold(row, rows)
            ),
            origin,
            target,
        )
        return [crossing, straight]

    def along(self, step, origin, target):
        if step < 0:
            return [self.add((step,), lambda c, r, n: r > 0, origin, target)]
        return [self.add((step,), lambda c, r, n: r < n - 1, origin, target)]


def each(routes, what, *args):
    for route in routes:
        getattr(route, what)(*args)


def pieces():
    height = SIDE // PIECES
    return [(b, k * height, height) for k in range(PIECES) for b in range(2)]


def halo_kernel(
    tile_ref, meta_ref, amps_ref, probe_ref, table_ref, region, metas, amps_out, probe_out, table_out, packed, blank, meta_blank, relay, local_sem, blank_sem,
    send_sem, recv_sem
):
    place = Place()
    roads = Roads(place, (send_sem, recv_sem), relay)
    upper, lower = pl.ds(0, SIDE), pl.ds(SIDE, SIDE)
    to_up, to_left, corners = [], [], []
    for i, (b, top, height) in enumerate(pieces()):
        mine, under = pl.ds(top, height), pl.ds(SIDE + top, height)
        to_up.append(roads.along(-8, packed.at[b, :, mine], region.at[b, :, under]))
        to_left.append(
            roads.across(-1, b, False, packed.at[b, :, mine], region.at[2 + b, :, mine])
        )
        corners.append(
            roads.across(-1, b, True, region.at[b, :, under], region.at[2 + b, :, under])
        )
    meta_right = roads.add((1,), lambda c, r, n: c < TILE_COLS - 1, meta_ref, metas.at[1])
    meta_down = roads.add((8,), lambda c, r, n: r < n - 1, meta_ref, metas.at[2])
    meta_relay = roads.add(
        (9,), lambda c, r, n: both(c < TILE_COLS - 1, r < n - 1), meta_ref, metas.at[3]
    )
    packs = [
        pltpu.make_async_copy(
            tile_ref.at[:, :, pl.ds(b * HALF, HALF)], packed.at[b], local_sem.at[3 + b]
        )
        for b in range(2)
    ]
    for copy in packs:
        copy.start()
    all_here = place.greet(roads.routes)
    assert roads.semaphores <= HALO_SEMS and roads.blocks <= HALO_BLOCKS, (
        roads.semaphores, roads.blocks
    )
    for copy in packs:
        copy.wait()

    own = [
        pltpu.make_async_copy(packed.at[b], region.at[b, :, upper], local_sem.at[b]) for b in range(2)
    ]
    own.append(pltpu.make_async_copy(meta_ref, metas.at[0], local_sem.at[2]))
    for i, (source, target) in enumerate(
        ((amps_ref, amps_out), (probe_ref, probe_out), (table_ref, table_out))
    ):
        own.append(pltpu.make_async_copy(source, target, local_sem.at[5 + i]))
    corner_there = both(place.right, place.down)
    above_there = both(place.left, place.up)
    blanks = []
    for b in range(2):
        for there, column, rows in (
            (place.right, 2 + b, upper),
            (place.down, b, lower),
            (corner_there, 2 + b, lower),
        ):
            blanks.append((there, blank, region.at[column, :, rows]))
    for i, there in enumerate((place.left, place.up, above_there)):
        blanks.append((there, meta_blank, metas.at[1 + i]))
    blanks = [
        (there, pltpu.make_async_copy(source, target, blank_sem.at[i]))
        for i, (there, source, target) in enumerate(blanks)
    ]

    all_here()
    for up, left in zip(to_up, to_left):
        each(up, "start")
        each(left, "start")
    meta_right.start()
    meta_down.start()
    meta_relay.start()
    blank[...] = jnp.zeros_like(blank)
    meta_blank[...] = jnp.zeros_like(meta_blank)
    for copy in own:
        copy.start()
    for there, copy in blanks:
        pl.when(jnp.logical_not(there))(copy.start)
    count = 2 * PIECES
    for step in range(count + LAG + LAG2):
        if step < count:
            each(to_left[step], "forward")
        if LAG <= step < count + LAG:
            each(to_up[step - LAG], "wait_recv")
            each(corners[step - LAG], "start")
        if step >= LAG + LAG2:
            each(corners[step - LAG - LAG2], "forward")
    for copy in own:
        copy.wait()
    for there, copy in blanks:
        pl.when(jnp.logical_not(there))(copy.wait)
    for group in (*to_left, *corners, [meta_right], [meta_down], [meta_relay]):
        each(group, "wait_recv")
    for group in (*to_up, *to_left, *corners, [meta_right], [meta_down], [meta_relay]):
        each(group, "wait_send")


HALO_SEMS = 60
HALO_BLOCKS = 16


def in_hbm(array):
    return pltpu.with_memory_space_constraint(array, pltpu.HBM)


def halo(tile, meta, amps, probe):
    V = pl.BlockSpec(memory_space=pltpu.VMEM)
    A = pl.BlockSpec(memory_space=pl.ANY)
    DMA = pltpu.SemaphoreType.DMA
    return pl.pallas_call(
        halo_kernel,
        out_shape=(
            jax.ShapeDtypeStruct((4, 2, 2 * SIDE, HALF), F32),
            jax.ShapeDtypeStruct((4, 8, HALF), jnp.int32),
            jax.ShapeDtypeStruct(amps.shape, BF16),
            jax.ShapeDtypeStruct(probe.shape, F32),
            jax.ShapeDtypeStruct((6, SIDE, SIDE), BF16),
        ),
        in_specs=[A, V, A, A, A],
        out_specs=(A, A, A, A, A),
        scratch_shapes=[
            pltpu.VMEM((2, 2, SIDE, HALF), F32),
            pltpu.VMEM((2, SIDE, HALF), F32),
            pltpu.VMEM((8, HALF), jnp.int32),
            pltpu.VMEM((HALO_BLOCKS, 2, SIDE // PIECES, HALF), F32),
            DMA((8,)),
            DMA((9,)),
            DMA((HALO_SEMS,)),
            DMA((HALO_SEMS,)),
        ],
        compiler_params=pltpu.CompilerParams(
            collective_id=0, has_side_effects=True, vmem_limit_bytes=12 << 20
        ),
        name="halo",
    )(in_hbm(tile), meta, in_hbm(amps), in_hbm(probe), in_hbm(dft_tables()))


def dft_tables():
    numbers = np.arange(SIDE)
    phases = (np.outer(numbers, numbers) % SIDE) * (2.0 * math.pi / SIDE)
    cosine = np.cos(phases) / math.sqrt(SIDE)
    minus_sine = -np.sin(phases) / math.sqrt(SIDE)
    halves = []
    for parity in range(2):
        c, m = cosine[:HALF, parity::2], minus_sine[:HALF, parity::2]
        halves.append(np.block([[c, -m], [m, c]]))
    tables = [cosine, minus_sine, *halves, *(half.T for half in halves)]
    return jnp.asarray(np.stack(tables), BF16)


def fit_kernel(
    meta_ref, region_ref, probe_ref, amps_ref, table_ref, left_ref, right_ref,
    fwd_ref, bwd_ref, columns, probes, rolled, wave, half, far,
):
    count = meta_ref[2, 0]
    groups = (count + GROUP - 1) // GROUP
    left_ref[...] = jnp.zeros_like(left_ref)
    right_ref[...] = jnp.zeros_like(right_ref)
    near_side, far_side = pl.ds(0, SIDE), pl.ds(SIDE, SIDE)
    for block in (near_side, far_side):
        fwd_ref[block, block] = table_ref[0]
        bwd_ref[block, block] = table_ref[0]
    fwd_ref[near_side, far_side] = -table_ref[1]
    fwd_ref[far_side, near_side] = table_ref[1]
    bwd_ref[near_side, far_side] = table_ref[1]
    bwd_ref[far_side, near_side] = -table_ref[1]
    for c in range(2):
        for b in range(2):
            columns[c, b] = probe_ref[c, :, b * HALF : (b + 1) * HALF]
        for parity in range(2):
            for b in range(2):
                probes[c, pl.ds(parity * HALF, HALF), pl.ds(b * HALF, HALF)] = columns[
                    c, b, pl.ds(parity, HALF, stride=2), :
                ]
    lanes = lax.broadcasted_iota(jnp.int32, (CHUNK, SIDE), 1)
    steps = HALF // CHUNK

    def make_wave(group, k):
        slot = GROUP * group + k
        row, col = meta_ref[0, slot], meta_ref[1, slot]
        inside = lanes >= col
        for parity in range(2):
            for step in range(steps):
                here = pl.ds(parity * HALF + step * CHUNK, CHUNK)
                there = pl.ds(row + parity + 2 * step * CHUNK, CHUNK, stride=2)
                probe_re = pltpu.roll(probes[0, here, :], col, 1)
                probe_im = pltpu.roll(probes[1, here, :], col, 1)
                rolled[k, 0, here, :] = probe_re
                rolled[k, 1, here, :] = probe_im
                part = []
                for c in range(2):
                    near = jnp.concatenate([region_ref[0, c, there, :], region_ref[1, c, there, :]], 1)
                    wide = jnp.concatenate([region_ref[2, c, there, :], region_ref[3, c, there, :]], 1)
                    part.append(jnp.where(inside, near, wide))
                wave[k, parity, pl.ds(step * CHUNK, CHUNK), :] = (
                    probe_re * part[0] - probe_im * part[1]
                ).astype(BF16)
                wave[k, parity, pl.ds(HALF + step * CHUNK, CHUNK), :] = (
                    probe_re * part[1] + probe_im * part[0]
                ).astype(BF16)

    def second(table, k):
        got = jnp.dot(half[k], table[...], preferred_element_type=F32)
        far[k, 0] = got[:, :SIDE]
        far[k, 1] = got[:, SIDE:]

    def forward(k):
        even = jnp.dot(table_ref[2], wave[k, 0], preferred_element_type=F32)
        odd = jnp.dot(table_ref[3], wave[k, 1], preferred_element_type=F32)
        for c in range(2):
            a, b = even[c * HALF : (c + 1) * HALF], odd[c * HALF : (c + 1) * HALF]
            half[k, pl.ds(0, HALF), pl.ds(c * SIDE, SIDE)] = (a + b).astype(BF16)
            half[k, pl.ds(HALF, HALF), pl.ds(c * SIDE, SIDE)] = (a - b).astype(BF16)

    def backward(k):
        for parity in range(2):
            got = jnp.dot(table_ref[4 + parity], wave[k, parity], preferred_element_type=F32)
            got = got.astype(BF16)
            rows = pl.ds(parity * HALF, HALF)
            half[k, rows, pl.ds(0, SIDE)] = got[:HALF]
            half[k, rows, pl.ds(SIDE, SIDE)] = got[HALF:]

    def correct(group, k):
        for step in range(steps):
            kept = []
            for top in range(2):
                here = pl.ds(top * HALF + step * CHUNK, CHUNK)
                far_re, far_im = far[k, 0, here, :], far[k, 1, here, :]
                measured = amps_ref[GROUP * group + k, here, :].astype(F32)
                inverse = jnp.minimum(lax.rsqrt(far_re * far_re + far_im * far_im), 2.0)
                retained = 1.0 - measured * inverse
                kept.append((far_re * retained, far_im * retained))
            for c in range(2):
                here = pl.ds(c * HALF + step * CHUNK, CHUNK)
                wave[k, 0, here, :] = (kept[0][c] + kept[1][c]).astype(BF16)
                wave[k, 1, here, :] = (kept[0][c] - kept[1][c]).astype(BF16)

    def deposit(group, k):
        slot = GROUP * group + k
        row, col = meta_ref[0, slot], meta_ref[1, slot]
        used = slot < count
        inside = lanes >= jnp.where(used, col, 2 * SIDE)
        outside = lanes < jnp.where(used, col, 0)
        for parity in range(2):
            for step in range(steps):
                here = pl.ds(parity * HALF + step * CHUNK, CHUNK)
                there = pl.ds(row + parity + 2 * step * CHUNK, CHUNK, stride=2)
                near_re, near_im = far[k, 0, here, :], far[k, 1, here, :]
                probe_re, probe_im = rolled[k, 0, here, :], rolled[k, 1, here, :]
                grads = (
                    probe_re * near_re + probe_im * near_im,
                    probe_re * near_im - probe_im * near_re,
                )
                for c in range(2):
                    near = jnp.where(inside, grads[c], 0.0)
                    wide = jnp.where(outside, grads[c], 0.0)
                    for b in range(2):
                        cols = slice(b * HALF, (b + 1) * HALF)
                        left_ref[b, c, there, :] += near[:, cols]
                        right_ref[b, c, there, :] += wide[:, cols]

    def body(group, carry):
        ks = range(GROUP)
        for k in ks:
            make_wave(group, k)
        for k in ks:
            forward(k)
        for k in ks:
            second(bwd_ref, k)
        for k in ks:
            correct(group, k)
        for k in ks:
            backward(k)
        for k in ks:
            second(fwd_ref, k)
        for k in ks:
            deposit(group, k)
        return carry

    lax.fori_loop(0, groups, body, 0)


def fit(meta, region, probe, amps, table):
    V = pl.BlockSpec(memory_space=pltpu.VMEM)
    S = pl.BlockSpec(memory_space=pltpu.SMEM)
    shape = jax.ShapeDtypeStruct((2, 2, 2 * SIDE, HALF), F32)
    return pl.pallas_call(
        fit_kernel,
        out_shape=(shape, shape),
        in_specs=[S, V, V, V, V],
        out_specs=(V, V),
        scratch_shapes=[
            pltpu.VMEM((2 * SIDE, 2 * SIDE), BF16),
            pltpu.VMEM((2 * SIDE, 2 * SIDE), BF16),
            pltpu.VMEM((2, 2, SIDE, HALF), F32),
            pltpu.VMEM((2, SIDE, SIDE), F32),
            pltpu.VMEM((GROUP, 2, SIDE, SIDE), F32),
            pltpu.VMEM((GROUP, 2, SIDE, SIDE), BF16),
            pltpu.VMEM((GROUP, SIDE, 2 * SIDE), BF16),
            pltpu.VMEM((GROUP, 2, SIDE, SIDE), F32),
        ],
        compiler_params=pltpu.CompilerParams(vmem_limit_bytes=24 << 20),
        name="fit",
    )(meta, region, probe, amps, table)


def join_kernel(
    metas, tile_ref, region, left_ref, right_ref, probe_ref, out_ref,
    corner, from_left, from_up, partner_tile, weights, rims, edge_right, edge_down,
    power, lighting, flow_x, flow_y, relay, local_sem, over_send, over_recv, send_sem, recv_sem,
):
    place = Place()
    partner = (1 - place.frame, place.tile)
    roads = Roads(place, (send_sem, recv_sem), relay)
    upper, lower = pl.ds(0, SIDE), pl.ds(SIDE, SIDE)
    edges = (
        pltpu.make_async_copy(region.at[2, :, upper], edge_right, local_sem.at[0]),
        pltpu.make_async_copy(region.at[pl.ds(0, 2), :, pl.ds(SIDE, 8)], edge_down, local_sem.at[1]),
    )
    for copy in edges:
        copy.start()

    corners, merged, plain = [], [], []
    for b, top, height in pieces():
        mine, under = pl.ds(top, height), pl.ds(SIDE + top, height)
        corners.append(
            roads.across(1, b, True, right_ref.at[b, :, under], corner.at[b, :, mine])
        )
        merged.append(roads.along(TILE_COLS, corner.at[b, :, mine], from_up.at[b, :, mine]))
        plain.append(
            roads.across(1, b, False, right_ref.at[b, :, mine], from_left.at[b, :, mine])
        )
    rim_right = roads.add((1,), lambda c, r, n: c < TILE_COLS - 1, rims.at[0], rims.at[1])
    rim_down = roads.add((TILE_COLS,), lambda c, r, n: r < n - 1, rims.at[2], rims.at[3])
    assert roads.semaphores <= JOIN_SEMS and roads.blocks <= JOIN_BLOCKS
    all_here = place.greet(roads.routes, partner)
    tile_over, weight_over = (
        pltpu.make_async_remote_copy(
            src_ref=source,
            dst_ref=target,
            send_sem=over_send.at[i],
            recv_sem=over_recv.at[i],
            device_id=partner,
            device_id_type=MESH,
        )
        for i, (source, target) in enumerate(
            ((tile_ref, partner_tile), (weights.at[0], weights.at[1]))
        )
    )

    all_here()
    tile_over.start()
    for sent in (*corners, *plain):
        each(sent, "start")

    @pl.when(jnp.logical_not(place.left))
    def _():
        from_left[...] = jnp.zeros_like(from_left)
        rims[1] = jnp.zeros((8, SIDE), F32)

    @pl.when(jnp.logical_not(place.up))
    def _():
        from_up[...] = jnp.zeros_like(from_up)
        rims[3] = jnp.zeros((8, SIDE), F32)

    rims[0] = jnp.zeros((8, SIDE), F32)
    rims[2] = jnp.zeros((8, SIDE), F32)

    for copy in edges:
        copy.wait()
    tile_over.wait_recv()
    lanes = lax.broadcasted_iota(jnp.int32, (SIDE, SIDE), 1)
    rows = lax.broadcasted_iota(jnp.int32, (SIDE, SIDE), 0)
    x_lives = jnp.logical_or(lanes < SIDE - 1, place.right)
    y_lives = jnp.logical_or(rows < SIDE - 1, place.down)
    total = jnp.full((SIDE, SIDE), smoothing, F32)
    for c in range(2):
        centre = tile_ref[c]
        beyond = pltpu.roll(edge_right[c], HALF - 1, 1)
        ahead = jnp.where(
            lanes == SIDE - 1, jnp.concatenate([beyond, beyond], 1), pltpu.roll(centre, SIDE - 1, 1)
        )
        diff_x = jnp.where(x_lives, ahead - centre, 0.0)
        below = jnp.concatenate([edge_down[0, c, 0:1, :], edge_down[1, c, 0:1, :]], 1)
        ahead = jnp.where(
            rows == SIDE - 1, jnp.broadcast_to(below, (SIDE, SIDE)), pltpu.roll(centre, SIDE - 1, 0)
        )
        diff_y = jnp.where(y_lives, ahead - centre, 0.0)
        diff_t = partner_tile[c] - centre
        flow_x[c] = diff_x
        flow_y[c] = diff_y
        total = total + diff_x * diff_x + diff_y * diff_y + diff_t * diff_t
    weight = lax.rsqrt(total)
    weights[0] = weight
    weight_over.start()
    for c in range(2):
        flow = weight * flow_x[c]
        flow_x[c] = flow
        rims[0, c : c + 1, :] = flow[:, HALF:].T[HALF - 1 : HALF, :]
        flow = weight * flow_y[c]
        flow_y[c] = flow
        rims[2, c : c + 1, :] = flow[SIDE - 1 : SIDE, :]
    rim_right.start()
    rim_down.start()

    lighted = probe_ref[0] * probe_ref[0] + probe_ref[1] * probe_ref[1]
    floor = damping * jnp.max(lighted) + 1e-6
    power[...] = jnp.zeros_like(power)
    for b in range(2):
        power[b, lower, :] = lighted[:, b * HALF : (b + 1) * HALF]
    lighting[...] = jnp.zeros_like(lighting)
    chunk_lanes = lax.broadcasted_iota(jnp.int32, (CHUNK, SIDE), 1)

    def lamp(number, carry):
        source, slot = number // SLOTS, number % SLOTS
        row, col = metas[source, 0, slot], metas[source, 1, slot]
        used = slot < metas[source, 2, 0]
        beside = source % 2 == 1
        start = SIDE + SIDE * (source // 2) - row
        low = jnp.where(beside, 0, jnp.where(used, col, 2 * SIDE))
        high = jnp.where(beside, jnp.where(used, col, 0), 2 * SIDE)
        lit = both(chunk_lanes >= low, chunk_lanes < high)
        for step in range(SIDE // CHUNK):
            here = pl.ds(step * CHUNK, CHUNK)
            there = pl.ds(start + step * CHUNK, CHUNK)
            light = jnp.concatenate([power[0, there, :], power[1, there, :]], 1)
            lighting[here, :] += jnp.where(lit, pltpu.roll(light, col, 1), 0.0)
        return carry

    count = 2 * PIECES
    lamps = 4 * SLOTS // count
    for step in range(count + LAG):
        if step < count:
            each(corners[step], "forward")
            lax.fori_loop(step * lamps, (step + 1) * lamps, lamp, 0)
        if step >= LAG:
            number = step - LAG
            b, top, height = pieces()[number]
            mine = pl.ds(top, height)
            each(corners[number], "wait_recv")

            @pl.when(both(place.down, place.left))
            def _():
                corner[b, :, mine] += left_ref[b, :, pl.ds(SIDE + top, height)]

            @pl.when(both(place.down, jnp.logical_not(place.left)))
            def _():
                corner[b, :, mine] = left_ref[b, :, pl.ds(SIDE + top, height)]

            each(merged[number], "start")
    for step in range(count):
        each(plain[step], "forward")

    weight_over.wait_recv()
    for sent in ([rim_right], [rim_down], *plain, *merged):
        each(sent, "wait_recv")
    for c in range(2):
        centre = tile_ref[c]
        diff_t = partner_tile[c] - centre
        rim = jnp.broadcast_to(rims[1, c : c + 1, :], (HALF, SIDE)).T
        rim = jnp.concatenate([rim, rim], 1)
        flow = flow_x[c]
        grad = jnp.where(lanes == 0, rim, pltpu.roll(flow, 1, 1)) - flow
        rim = jnp.broadcast_to(rims[3, c : c + 1, :], (SIDE, SIDE))
        flow = flow_y[c]
        grad = grad + jnp.where(rows == 0, rim, pltpu.roll(flow, 1, 0)) - flow
        grad = grad - (weights[0] + weights[1]) * diff_t
        fit = jnp.concatenate(
            [left_ref[b, c, upper, :] + from_left[b, c] + from_up[b, c] for b in range(2)], 1
        )
        out_ref[c] = centre - fit / (lighting[...] + floor) - variation_weight * grad
    tile_over.wait_send()
    weight_over.wait_send()
    for sent in ([rim_right], [rim_down], *corners, *plain, *merged):
        each(sent, "wait_send")


JOIN_SEMS = 60
JOIN_BLOCKS = 16
SLOTS = 16


def join(metas, tile, region, left, right, probe):
    V = pl.BlockSpec(memory_space=pltpu.VMEM)
    S = pl.BlockSpec(memory_space=pltpu.SMEM)
    block = (2, SIDE, HALF)
    return pl.pallas_call(
        join_kernel,
        out_shape=jax.ShapeDtypeStruct((2, SIDE, SIDE), F32),
        in_specs=[S, V, pl.BlockSpec(memory_space=pl.ANY), V, V, V],
        out_specs=V,
        scratch_shapes=[
            pltpu.VMEM((2, *block), F32),
            pltpu.VMEM((2, *block), F32),
            pltpu.VMEM((2, *block), F32),
            pltpu.VMEM((2, SIDE, SIDE), F32),
            pltpu.VMEM((2, SIDE, SIDE), F32),
            pltpu.VMEM((4, 8, SIDE), F32),
            pltpu.VMEM(block, F32),
            pltpu.VMEM((2, 2, 8, HALF), F32),
            pltpu.VMEM((2, 3 * SIDE, HALF), F32),
            pltpu.VMEM((SIDE, SIDE), F32),
            pltpu.VMEM((2, SIDE, SIDE), F32),
            pltpu.VMEM((2, SIDE, SIDE), F32),
            pltpu.VMEM((JOIN_BLOCKS, 2, SIDE // PIECES, HALF), F32),
            pltpu.SemaphoreType.DMA((2,)),
            pltpu.SemaphoreType.DMA((2,)),
            pltpu.SemaphoreType.DMA((2,)),
            pltpu.SemaphoreType.DMA((JOIN_SEMS,)),
            pltpu.SemaphoreType.DMA((JOIN_SEMS,)),
        ],
        compiler_params=pltpu.CompilerParams(
            collective_id=1, has_side_effects=True, vmem_limit_bytes=20 << 20
        ),
        name="join",
    )(metas, tile, region, left, right, probe)


def local(object_tiles, probe_field, amplitudes, offsets, counts):
    tile = object_tiles[0, 0]
    slots = amplitudes.shape[1]
    meta = jnp.concatenate([offsets[0].T, jnp.broadcast_to(counts, (6, slots))], 0)
    meta = jnp.pad(meta, ((0, 0), (0, HALF - slots)))
    region, metas, amps, probe, table = halo(tile, meta, amplitudes[0], probe_field)
    left, right = fit(meta, region, probe, amps, table)
    return join(metas, tile, region, left, right, probe)[None, None]


def solution(mesh):
    return jax.shard_map(
        local,
        mesh=mesh,
        in_specs=(
            P("frame", "tile", None, None, None),
            P(),
            P("frame", "tile", None, None),
            P("frame", "tile", None),
            P("frame", "tile"),
        ),
        out_specs=P("frame", "tile", None, None, None),
        check_vma=False,
    )
```

```python
import functools
import math

import jax
import jax.numpy as jnp
import numpy as np
from jax import lax
from jax.experimental import pallas as pl
from jax.experimental.pallas import tpu as pltpu
from jax.sharding import PartitionSpec as P

TILE_COLS = 8
SIDE = 256
HALF = 128
CHUNK = 32
GROUP = 4
PIECES = 4
LAG = 3
LAG2 = 2
F32, BF16 = jnp.float32, jnp.bfloat16
MESH = pl.DeviceIdType.MESH

damping = 0.1
variation_weight = 0.2
smoothing = 0.25


def both(a, b):
    return jnp.logical_and(a, b)


class Place:
    def __init__(self):
        self.frame = lax.axis_index("frame")
        self.tile = lax.axis_index("tile")
        self.tiles = lax.axis_size("tile")
        column, row = self.tile % TILE_COLS, self.tile // TILE_COLS
        self.left = column > 0
        self.right = column < TILE_COLS - 1
        self.up = row > 0
        self.down = row < self.tiles // TILE_COLS - 1

    def holds(self, source, step):
        tile = self.tile - step
        there = both(tile >= 0, tile < self.tiles)
        return both(there, source(tile % TILE_COLS, tile // TILE_COLS, self.tiles // TILE_COLS))

    def greet(self, routes, partner=None):
        barrier = pltpu.get_barrier_semaphore()
        before, after = {}, {}
        for route in routes:
            for h, step in enumerate(route.hops):
                for known, role in ((after, route.roles[h]), (before, route.roles[h + 1])):
                    known[step] = jnp.logical_or(known[step], role) if step in known else role
        for step, there in before.items():

            @pl.when(there)
            def _(step=step):
                device = (self.frame, self.tile - step)
                pl.semaphore_signal(barrier, inc=1, device_id=device, device_id_type=MESH)

        total = jnp.int32(0)
        for there in after.values():
            total = total + there.astype(jnp.int32)
        if partner is not None:
            total = total + 1
            pl.semaphore_signal(barrier, inc=1, device_id=partner, device_id_type=MESH)
        return lambda: pl.semaphore_wait(barrier, total)


class Route:
    def __init__(self, place, sems, index, hops, source, origin, target, relays=()):
        assert len(relays) == len(hops) - 1
        steps = [sum(hops[:h]) for h in range(len(hops) + 1)]
        self.hops = hops
        self.roles = [place.holds(source, step) for step in steps]
        stops = [origin, *relays, target]
        self.copies = [
            functools.partial(
                pltpu.make_async_remote_copy,
                src_ref=stops[h],
                dst_ref=stops[h + 1],
                send_sem=sems[0].at[index + h],
                recv_sem=sems[1].at[index + h],
                device_id=(place.frame, place.tile + hops[h]),
                device_id_type=MESH,
            )
            for h in range(len(hops))
        ]

    def start(self):
        @pl.when(self.roles[0])
        def _():
            self.copies[0]().start()

    def forward(self, h=1):
        if h >= len(self.hops):
            return

        @pl.when(self.roles[h])
        def _():
            self.copies[h - 1]().wait_recv()
            self.copies[h]().start()

    def wait_recv(self):
        @pl.when(self.roles[-1])
        def _():
            self.copies[-1]().wait_recv()

    def wait_send(self):
        for h in range(len(self.hops)):

            @pl.when(self.roles[h])
            def _(h=h):
                self.copies[h]().wait_send()


class Roads:
    def __init__(self, place, sems, relay):
        self.place, self.sems, self.relay = place, sems, relay
        self.semaphores = 0
        self.blocks = 0
        self.routes = []

    def add(self, hops, source, origin, target):
        relays = [self.relay.at[self.blocks + h] for h in range(len(hops) - 1)]
        route = Route(self.place, self.sems, self.semaphores, hops, source, origin, target, relays)
        self.semaphores += len(hops)
        self.blocks += len(hops) - 1
        self.routes.append(route)
        return route

    def across(self, step, half, tall, origin, target):
        def rows_hold(row, rows):
            return row < rows - 1 if tall else row >= 0

        start, last = (4, 0) if step < 0 else (3, TILE_COLS - 1)
        hops = (-4, 3) if step < 0 else (-3, 4)
        crossing = self.add(
            hops if half == 0 else hops[::-1],
            lambda column, row, rows: both(column == start, rows_hold(row, rows)),
            origin,
            target,
        )
        straight = self.add(
            (step,),
            lambda column, row, rows: both(
                both(column != start, column != last), rows_hold(row, rows)
            ),
            origin,
            target,
        )
        return [crossing, straight]

    def along(self, step, origin, target):
        if step < 0:
            return [self.add((step,), lambda c, r, n: r > 0, origin, target)]
        return [self.add((step,), lambda c, r, n: r < n - 1, origin, target)]


def each(routes, what, *args):
    for route in routes:
        getattr(route, what)(*args)


def pieces():
    height = SIDE // PIECES
    return [(b, k * height, height) for k in range(PIECES) for b in range(2)]


def halo_kernel(
    tile_ref, meta_ref, amps_ref, probe_ref, table_ref, region, metas, amps_out, probe_out, table_out, packed, blank, meta_blank, relay, local_sem, blank_sem,
    send_sem, recv_sem
):
    place = Place()
    roads = Roads(place, (send_sem, recv_sem), relay)
    upper, lower = pl.ds(0, SIDE), pl.ds(SIDE, SIDE)
    to_up, to_left, corners = [], [], []
    for i, (b, top, height) in enumerate(pieces()):
        mine, under = pl.ds(top, height), pl.ds(SIDE + top, height)
        to_up.append(roads.along(-8, packed.at[b, :, mine], region.at[b, :, under]))
        to_left.append(
            roads.across(-1, b, False, packed.at[b, :, mine], region.at[2 + b, :, mine])
        )
        corners.append(
            roads.across(-1, b, True, region.at[b, :, under], region.at[2 + b, :, under])
        )
    meta_right = roads.add((1,), lambda c, r, n: c < TILE_COLS - 1, meta_ref, metas.at[1])
    meta_down = roads.add((8,), lambda c, r, n: r < n - 1, meta_ref, metas.at[2])
    meta_relay = roads.add(
        (9,), lambda c, r, n: both(c < TILE_COLS - 1, r < n - 1), meta_ref, metas.at[3]
    )
    packs = [
        pltpu.make_async_copy(
            tile_ref.at[:, :, pl.ds(b * HALF, HALF)], packed.at[b], local_sem.at[3 + b]
        )
        for b in range(2)
    ]
    for copy in packs:
        copy.start()
    all_here = place.greet(roads.routes)
    assert roads.semaphores <= HALO_SEMS and roads.blocks <= HALO_BLOCKS, (
        roads.semaphores, roads.blocks
    )
    for copy in packs:
        copy.wait()

    own = [
        pltpu.make_async_copy(packed.at[b], region.at[b, :, upper], local_sem.at[b]) for b in range(2)
    ]
    own.append(pltpu.make_async_copy(meta_ref, metas.at[0], local_sem.at[2]))
    for i, (source, target) in enumerate(
        ((amps_ref, amps_out), (probe_ref, probe_out), (table_ref, table_out))
    ):
        own.append(pltpu.make_async_copy(source, target, local_sem.at[5 + i]))
    corner_there = both(place.right, place.down)
    above_there = both(place.left, place.up)
    blanks = []
    for b in range(2):
        for there, column, rows in (
            (place.right, 2 + b, upper),
            (place.down, b, lower),
            (corner_there, 2 + b, lower),
        ):
            blanks.append((there, blank, region.at[column, :, rows]))
    for i, there in enumerate((place.left, place.up, above_there)):
        blanks.append((there, meta_blank, metas.at[1 + i]))
    blanks = [
        (there, pltpu.make_async_copy(source, target, blank_sem.at[i]))
        for i, (there, source, target) in enumerate(blanks)
    ]

    all_here()
    for up, left in zip(to_up, to_left):
        each(up, "start")
        each(left, "start")
    meta_right.start()
    meta_down.start()
    meta_relay.start()
    blank[...] = jnp.zeros_like(blank)
    meta_blank[...] = jnp.zeros_like(meta_blank)
    for copy in own:
        copy.start()
    for there, copy in blanks:
        pl.when(jnp.logical_not(there))(copy.start)
    count = 2 * PIECES
    for step in range(count + LAG + LAG2):
        if step < count:
            each(to_left[step], "forward")
        if LAG <= step < count + LAG:
            each(to_up[step - LAG], "wait_recv")
            each(corners[step - LAG], "start")
        if step >= LAG + LAG2:
            each(corners[step - LAG - LAG2], "forward")
    for copy in own:
        copy.wait()
    for there, copy in blanks:
        pl.when(jnp.logical_not(there))(copy.wait)
    for group in (*to_left, *corners, [meta_right], [meta_down], [meta_relay]):
        each(group, "wait_recv")
    for group in (*to_up, *to_left, *corners, [meta_right], [meta_down], [meta_relay]):
        each(group, "wait_send")


HALO_SEMS = 60
HALO_BLOCKS = 16


def in_hbm(array):
    return pltpu.with_memory_space_constraint(array, pltpu.HBM)


def halo(tile, meta, amps, probe):
    V = pl.BlockSpec(memory_space=pltpu.VMEM)
    A = pl.BlockSpec(memory_space=pl.ANY)
    DMA = pltpu.SemaphoreType.DMA
    return pl.pallas_call(
        halo_kernel,
        out_shape=(
            jax.ShapeDtypeStruct((4, 2, 2 * SIDE, HALF), F32),
            jax.ShapeDtypeStruct((4, 8, HALF), jnp.int32),
            jax.ShapeDtypeStruct(amps.shape, BF16),
            jax.ShapeDtypeStruct(probe.shape, F32),
            jax.ShapeDtypeStruct((6, SIDE, SIDE), BF16),
        ),
        in_specs=[A, V, A, A, A],
        out_specs=(A, A, A, A, A),
        scratch_shapes=[
            pltpu.VMEM((2, 2, SIDE, HALF), F32),
            pltpu.VMEM((2, SIDE, HALF), F32),
            pltpu.VMEM((8, HALF), jnp.int32),
            pltpu.VMEM((HALO_BLOCKS, 2, SIDE // PIECES, HALF), F32),
            DMA((8,)),
            DMA((9,)),
            DMA((HALO_SEMS,)),
            DMA((HALO_SEMS,)),
        ],
        compiler_params=pltpu.CompilerParams(
            collective_id=0, has_side_effects=True, vmem_limit_bytes=12 << 20
        ),
        name="halo",
    )(in_hbm(tile), meta, in_hbm(amps), in_hbm(probe), in_hbm(dft_tables()))


def dft_tables():
    numbers = np.arange(SIDE)
    phases = (np.outer(numbers, numbers) % SIDE) * (2.0 * math.pi / SIDE)
    cosine = np.cos(phases) / math.sqrt(SIDE)
    minus_sine = -np.sin(phases) / math.sqrt(SIDE)
    halves = []
    for parity in range(2):
        c, m = cosine[:HALF, parity::2], minus_sine[:HALF, parity::2]
        halves.append(np.block([[c, -m], [m, c]]))
    tables = [cosine, minus_sine, *halves, *(half.T for half in halves)]
    return jnp.asarray(np.stack(tables), BF16)


def fit_kernel(
    meta_ref, region_ref, probe_ref, amps_ref, table_ref, left_ref, right_ref,
    fwd_ref, bwd_ref, columns, probes, rolled, wave, half, far,
):
    count = meta_ref[2, 0]
    groups = (count + GROUP - 1) // GROUP
    left_ref[...] = jnp.zeros_like(left_ref)
    right_ref[...] = jnp.zeros_like(right_ref)
    near_side, far_side = pl.ds(0, SIDE), pl.ds(SIDE, SIDE)
    for block in (near_side, far_side):
        fwd_ref[block, block] = table_ref[0]
        bwd_ref[block, block] = table_ref[0]
    fwd_ref[near_side, far_side] = -table_ref[1]
    fwd_ref[far_side, near_side] = table_ref[1]
    bwd_ref[near_side, far_side] = table_ref[1]
    bwd_ref[far_side, near_side] = -table_ref[1]
    for c in range(2):
        for b in range(2):
            columns[c, b] = probe_ref[c, :, b * HALF : (b + 1) * HALF]
        for parity in range(2):
            for b in range(2):
                probes[c, pl.ds(parity * HALF, HALF), pl.ds(b * HALF, HALF)] = columns[
                    c, b, pl.ds(parity, HALF, stride=2), :
                ]
    lanes = lax.broadcasted_iota(jnp.int32, (CHUNK, SIDE), 1)
    steps = HALF // CHUNK

    def make_wave(group, k):
        slot = GROUP * group + k
        row, col = meta_ref[0, slot], meta_ref[1, slot]
        inside = lanes >= col
        for parity in range(2):
            for step in range(steps):
                here = pl.ds(parity * HALF + step * CHUNK, CHUNK)
                there = pl.ds(row + parity + 2 * step * CHUNK, CHUNK, stride=2)
                probe_re = pltpu.roll(probes[0, here, :], col, 1)
                probe_im = pltpu.roll(probes[1, here, :], col, 1)
                rolled[k, 0, here, :] = probe_re
                rolled[k, 1, here, :] = probe_im
                part = []
                for c in range(2):
                    near = jnp.concatenate([region_ref[0, c, there, :], region_ref[1, c, there, :]], 1)
                    wide = jnp.concatenate([region_ref[2, c, there, :], region_ref[3, c, there, :]], 1)
                    part.append(jnp.where(inside, near, wide))
                wave[k, parity, pl.ds(step * CHUNK, CHUNK), :] = (
                    probe_re * part[0] - probe_im * part[1]
                ).astype(BF16)
                wave[k, parity, pl.ds(HALF + step * CHUNK, CHUNK), :] = (
                    probe_re * part[1] + probe_im * part[0]
                ).astype(BF16)

    def second(table, k):
        got = jnp.dot(half[k], table[...], preferred_element_type=F32)
        far[k, 0] = got[:, :SIDE]
        far[k, 1] = got[:, SIDE:]

    def forward(k):
        even = jnp.dot(table_ref[2], wave[k, 0], preferred_element_type=F32)
        odd = jnp.dot(table_ref[3], wave[k, 1], preferred_element_type=F32)
        for c in range(2):
            a, b = even[c * HALF : (c + 1) * HALF], odd[c * HALF : (c + 1) * HALF]
            half[k, pl.ds(0, HALF), pl.ds(c * SIDE, SIDE)] = (a + b).astype(BF16)
            half[k, pl.ds(HALF, HALF), pl.ds(c * SIDE, SIDE)] = (a - b).astype(BF16)

    def backward(k):
        for parity in range(2):
            got = jnp.dot(table_ref[4 + parity], wave[k, parity], preferred_element_type=F32)
            got = got.astype(BF16)
            rows = pl.ds(parity * HALF, HALF)
            half[k, rows, pl.ds(0, SIDE)] = got[:HALF]
            half[k, rows, pl.ds(SIDE, SIDE)] = got[HALF:]

    def correct(group, k):
        for step in range(steps):
            kept = []
            for top in range(2):
                here = pl.ds(top * HALF + step * CHUNK, CHUNK)
                far_re, far_im = far[k, 0, here, :], far[k, 1, here, :]
                measured = amps_ref[GROUP * group + k, here, :].astype(F32)
                inverse = jnp.minimum(lax.rsqrt(far_re * far_re + far_im * far_im), 2.0)
                retained = 1.0 - measured * inverse
                kept.append((far_re * retained, far_im * retained))
            for c in range(2):
                here = pl.ds(c * HALF + step * CHUNK, CHUNK)
                wave[k, 0, here, :] = (kept[0][c] + kept[1][c]).astype(BF16)
                wave[k, 1, here, :] = (kept[0][c] - kept[1][c]).astype(BF16)

    def deposit(group, k):
        slot = GROUP * group + k
        row, col = meta_ref[0, slot], meta_ref[1, slot]
        used = slot < count
        inside = lanes >= jnp.where(used, col, 2 * SIDE)
        outside = lanes < jnp.where(used, col, 0)
        for parity in range(2):
            for step in range(steps):
                here = pl.ds(parity * HALF + step * CHUNK, CHUNK)
                there = pl.ds(row + parity + 2 * step * CHUNK, CHUNK, stride=2)
                near_re, near_im = far[k, 0, here, :], far[k, 1, here, :]
                probe_re, probe_im = rolled[k, 0, here, :], rolled[k, 1, here, :]
                grads = (
                    probe_re * near_re + probe_im * near_im,
                    probe_re * near_im - probe_im * near_re,
                )
                for c in range(2):
                    near = jnp.where(inside, grads[c], 0.0)
                    wide = jnp.where(outside, grads[c], 0.0)
                    for b in range(2):
                        cols = slice(b * HALF, (b + 1) * HALF)
                        left_ref[b, c, there, :] += near[:, cols]
                        right_ref[b, c, there, :] += wide[:, cols]

    def body(group, carry):
        ks = range(GROUP)
        for k in ks:
            make_wave(group, k)
        for k in ks:
            forward(k)
        for k in ks:
            second(bwd_ref, k)
        for k in ks:
            correct(group, k)
        for k in ks:
            backward(k)
        for k in ks:
            second(fwd_ref, k)
        for k in ks:
            deposit(group, k)
        return carry

    lax.fori_loop(0, groups, body, 0)


def fit(meta, region, probe, amps, table):
    V = pl.BlockSpec(memory_space=pltpu.VMEM)
    S = pl.BlockSpec(memory_space=pltpu.SMEM)
    shape = jax.ShapeDtypeStruct((2, 2, 2 * SIDE, HALF), F32)
    return pl.pallas_call(
        fit_kernel,
        out_shape=(shape, shape),
        in_specs=[S, V, V, V, V],
        out_specs=(V, V),
        scratch_shapes=[
            pltpu.VMEM((2 * SIDE, 2 * SIDE), BF16),
            pltpu.VMEM((2 * SIDE, 2 * SIDE), BF16),
            pltpu.VMEM((2, 2, SIDE, HALF), F32),
            pltpu.VMEM((2, SIDE, SIDE), F32),
            pltpu.VMEM((GROUP, 2, SIDE, SIDE), F32),
            pltpu.VMEM((GROUP, 2, SIDE, SIDE), BF16),
            pltpu.VMEM((GROUP, SIDE, 2 * SIDE), BF16),
            pltpu.VMEM((GROUP, 2, SIDE, SIDE), F32),
        ],
        compiler_params=pltpu.CompilerParams(vmem_limit_bytes=24 << 20),
        name="fit",
    )(meta, region, probe, amps, table)


def join_kernel(
    metas, tile_ref, region, left_ref, right_ref, probe_ref, out_ref,
    corner, from_left, from_up, partner_tile, weights, rims, edge_right, edge_down,
    power, lighting, flow_x, flow_y, relay, local_sem, over_send, over_recv, send_sem, recv_sem,
):
    place = Place()
    partner = (1 - place.frame, place.tile)
    roads = Roads(place, (send_sem, recv_sem), relay)
    upper, lower = pl.ds(0, SIDE), pl.ds(SIDE, SIDE)
    edges = (
        pltpu.make_async_copy(region.at[2, :, upper], edge_right, local_sem.at[0]),
        pltpu.make_async_copy(region.at[pl.ds(0, 2), :, pl.ds(SIDE, 8)], edge_down, local_sem.at[1]),
    )
    for copy in edges:
        copy.start()

    corners, merged, plain = [], [], []
    for b, top, height in pieces():
        mine, under = pl.ds(top, height), pl.ds(SIDE + top, height)
        corners.append(
            roads.across(1, b, True, right_ref.at[b, :, under], corner.at[b, :, mine])
        )
        merged.append(roads.along(TILE_COLS, corner.at[b, :, mine], from_up.at[b, :, mine]))
        plain.append(
            roads.across(1, b, False, right_ref.at[b, :, mine], from_left.at[b, :, mine])
        )
    rim_right = roads.add((1,), lambda c, r, n: c < TILE_COLS - 1, rims.at[0], rims.at[1])
    rim_down = roads.add((TILE_COLS,), lambda c, r, n: r < n - 1, rims.at[2], rims.at[3])
    assert roads.semaphores <= JOIN_SEMS and roads.blocks <= JOIN_BLOCKS
    all_here = place.greet(roads.routes, partner)
    tile_over, weight_over = (
        pltpu.make_async_remote_copy(
            src_ref=source,
            dst_ref=target,
            send_sem=over_send.at[i],
            recv_sem=over_recv.at[i],
            device_id=partner,
            device_id_type=MESH,
        )
        for i, (source, target) in enumerate(
            ((tile_ref, partner_tile), (weights.at[0], weights.at[1]))
        )
    )

    all_here()
    tile_over.start()
    for sent in (*corners, *plain):
        each(sent, "start")

    @pl.when(jnp.logical_not(place.left))
    def _():
        from_left[...] = jnp.zeros_like(from_left)
        rims[1] = jnp.zeros((8, SIDE), F32)

    @pl.when(jnp.logical_not(place.up))
    def _():
        from_up[...] = jnp.zeros_like(from_up)
        rims[3] = jnp.zeros((8, SIDE), F32)

    rims[0] = jnp.zeros((8, SIDE), F32)
    rims[2] = jnp.zeros((8, SIDE), F32)

    for copy in edges:
        copy.wait()
    tile_over.wait_recv()
    lanes = lax.broadcasted_iota(jnp.int32, (SIDE, SIDE), 1)
    rows = lax.broadcasted_iota(jnp.int32, (SIDE, SIDE), 0)
    x_lives = jnp.logical_or(lanes < SIDE - 1, place.right)
    y_lives = jnp.logical_or(rows < SIDE - 1, place.down)
    total = jnp.full((SIDE, SIDE), smoothing, F32)
    for c in range(2):
        centre = tile_ref[c]
        beyond = pltpu.roll(edge_right[c], HALF - 1, 1)
        ahead = jnp.where(
            lanes == SIDE - 1, jnp.concatenate([beyond, beyond], 1), pltpu.roll(centre, SIDE - 1, 1)
        )
        diff_x = jnp.where(x_lives, ahead - centre, 0.0)
        below = jnp.concatenate([edge_down[0, c, 0:1, :], edge_down[1, c, 0:1, :]], 1)
        ahead = jnp.where(
            rows == SIDE - 1, jnp.broadcast_to(below, (SIDE, SIDE)), pltpu.roll(centre, SIDE - 1, 0)
        )
        diff_y = jnp.where(y_lives, ahead - centre, 0.0)
        diff_t = partner_tile[c] - centre
        flow_x[c] = diff_x
        flow_y[c] = diff_y
        total = total + diff_x * diff_x + diff_y * diff_y + diff_t * diff_t
    weight = lax.rsqrt(total)
    weights[0] = weight
    weight_over.start()
    for c in range(2):
        flow = weight * flow_x[c]
        flow_x[c] = flow
        rims[0, c : c + 1, :] = flow[:, HALF:].T[HALF - 1 : HALF, :]
        flow = weight * flow_y[c]
        flow_y[c] = flow
        rims[2, c : c + 1, :] = flow[SIDE - 1 : SIDE, :]
    rim_right.start()
    rim_down.start()

    lighted = probe_ref[0] * probe_ref[0] + probe_ref[1] * probe_ref[1]
    floor = damping * jnp.max(lighted) + 1e-6
    power[...] = jnp.zeros_like(power)
    for b in range(2):
        power[b, lower, :] = lighted[:, b * HALF : (b + 1) * HALF]
    lighting[...] = jnp.zeros_like(lighting)
    chunk_lanes = lax.broadcasted_iota(jnp.int32, (CHUNK, SIDE), 1)

    def lamp(number, carry):
        source, slot = number // SLOTS, number % SLOTS
        row, col = metas[source, 0, slot], metas[source, 1, slot]
        used = slot < metas[source, 2, 0]
        beside = source % 2 == 1
        start = SIDE + SIDE * (source // 2) - row
        low = jnp.where(beside, 0, jnp.where(used, col, 2 * SIDE))
        high = jnp.where(beside, jnp.where(used, col, 0), 2 * SIDE)
        lit = both(chunk_lanes >= low, chunk_lanes < high)
        for step in range(SIDE // CHUNK):
            here = pl.ds(step * CHUNK, CHUNK)
            there = pl.ds(start + step * CHUNK, CHUNK)
            light = jnp.concatenate([power[0, there, :], power[1, there, :]], 1)
            lighting[here, :] += jnp.where(lit, pltpu.roll(light, col, 1), 0.0)
        return carry

    count = 2 * PIECES
    ring = place.tile % 4
    early = jnp.where(jnp.logical_or(ring == 0, ring == 3), 4 * SLOTS // count, 0)
    for step in range(count + LAG):
        if step < count:
            each(corners[step], "forward")
            lax.fori_loop(step * early, (step + 1) * early, lamp, 0)
        if step >= LAG:
            number = step - LAG
            b, top, height = pieces()[number]
            mine = pl.ds(top, height)
            each(corners[number], "wait_recv")

            @pl.when(both(place.down, place.left))
            def _():
                corner[b, :, mine] += left_ref[b, :, pl.ds(SIDE + top, height)]

            @pl.when(both(place.down, jnp.logical_not(place.left)))
            def _():
                corner[b, :, mine] = left_ref[b, :, pl.ds(SIDE + top, height)]

            each(merged[number], "start")
    for step in range(count):
        each(plain[step], "forward")
    lax.fori_loop(count * early, 4 * SLOTS, lamp, 0)

    weight_over.wait_recv()
    for sent in ([rim_right], [rim_down], *plain, *merged):
        each(sent, "wait_recv")
    for c in range(2):
        centre = tile_ref[c]
        diff_t = partner_tile[c] - centre
        rim = jnp.broadcast_to(rims[1, c : c + 1, :], (HALF, SIDE)).T
        rim = jnp.concatenate([rim, rim], 1)
        flow = flow_x[c]
        grad = jnp.where(lanes == 0, rim, pltpu.roll(flow, 1, 1)) - flow
        rim = jnp.broadcast_to(rims[3, c : c + 1, :], (SIDE, SIDE))
        flow = flow_y[c]
        grad = grad + jnp.where(rows == 0, rim, pltpu.roll(flow, 1, 0)) - flow
        grad = grad - (weights[0] + weights[1]) * diff_t
        fit = jnp.concatenate(
            [left_ref[b, c, upper, :] + from_left[b, c] + from_up[b, c] for b in range(2)], 1
        )
        out_ref[c] = centre - fit / (lighting[...] + floor) - variation_weight * grad
    tile_over.wait_send()
    weight_over.wait_send()
    for sent in ([rim_right], [rim_down], *corners, *plain, *merged):
        each(sent, "wait_send")


JOIN_SEMS = 60
JOIN_BLOCKS = 16
SLOTS = 16


def join(metas, tile, region, left, right, probe):
    V = pl.BlockSpec(memory_space=pltpu.VMEM)
    S = pl.BlockSpec(memory_space=pltpu.SMEM)
    block = (2, SIDE, HALF)
    return pl.pallas_call(
        join_kernel,
        out_shape=jax.ShapeDtypeStruct((2, SIDE, SIDE), F32),
        in_specs=[S, V, pl.BlockSpec(memory_space=pl.ANY), V, V, V],
        out_specs=V,
        scratch_shapes=[
            pltpu.VMEM((2, *block), F32),
            pltpu.VMEM((2, *block), F32),
            pltpu.VMEM((2, *block), F32),
            pltpu.VMEM((2, SIDE, SIDE), F32),
            pltpu.VMEM((2, SIDE, SIDE), F32),
            pltpu.VMEM((4, 8, SIDE), F32),
            pltpu.VMEM(block, F32),
            pltpu.VMEM((2, 2, 8, HALF), F32),
            pltpu.VMEM((2, 3 * SIDE, HALF), F32),
            pltpu.VMEM((SIDE, SIDE), F32),
            pltpu.VMEM((2, SIDE, SIDE), F32),
            pltpu.VMEM((2, SIDE, SIDE), F32),
            pltpu.VMEM((JOIN_BLOCKS, 2, SIDE // PIECES, HALF), F32),
            pltpu.SemaphoreType.DMA((2,)),
            pltpu.SemaphoreType.DMA((2,)),
            pltpu.SemaphoreType.DMA((2,)),
            pltpu.SemaphoreType.DMA((JOIN_SEMS,)),
            pltpu.SemaphoreType.DMA((JOIN_SEMS,)),
        ],
        compiler_params=pltpu.CompilerParams(
            collective_id=1, has_side_effects=True, vmem_limit_bytes=20 << 20
        ),
        name="join",
    )(metas, tile, region, left, right, probe)


def local(object_tiles, probe_field, amplitudes, offsets, counts):
    tile = object_tiles[0, 0]
    slots = amplitudes.shape[1]
    meta = jnp.concatenate([offsets[0].T, jnp.broadcast_to(counts, (6, slots))], 0)
    meta = jnp.pad(meta, ((0, 0), (0, HALF - slots)))
    region, metas, amps, probe, table = halo(tile, meta, amplitudes[0], probe_field)
    left, right = fit(meta, region, probe, amps, table)
    return join(metas, tile, region, left, right, probe)[None, None]


def solution(mesh):
    return jax.shard_map(
        local,
        mesh=mesh,
        in_specs=(
            P("frame", "tile", None, None, None),
            P(),
            P("frame", "tile", None, None),
            P("frame", "tile", None),
            P("frame", "tile"),
        ),
        out_specs=P("frame", "tile", None, None, None),
        check_vma=False,
    )
```
